32 devices in a mesh: rng: 8 (over z, x), az: 4 (over y, core).
Axes of the slice: x: 2, y: 2, z: 4, core: 2. Of those that a mesh axis runs over, the one named last changes fastest.
Arguments:
- sar_image: float32 [2, 512, 16384], P(None, 'rng', 'az'), may hold values from -6 to 6
- strong_index: int32 [256], P('rng'), may hold values from 0 to 511, as said below
- shifts: int32 [256], P('rng'), may hold values from 0 to 16383
- widths: int32 [256], P('rng'), may hold values from 256 to 2048
Outputs:
- focused_image: float32 [2, 512, 16384], P(None, 'rng', 'az')
- phase_error: float32 [16384], P('az')
The draws below stay inside these ranges and needn't reach their ends.
Inputs may be any that keep to these rules, and one draw needn't show every extreme that they name: `strong_index`: entries r * 32 to (r + 1) * 32 - 1 are distinct range bins of the block r * 64 to (r + 1) * 64 - 1.
All inputs are finite; a program needn't handle non-finite values.
Results may differ from the reference program's by a relative error of at most 0.0003.
Values sent between devices are 32-bit elements; how exact they have to be, the bound alone decides.
A program may use at most 64 MiB of HBM per device.

```python
import jax
import jax.numpy as jnp

PULSES = 16384
RNG_DEV = 64
STRONG_DEV = 32
ITERS = 2
RANGE = 512
STRONG_TOTAL = 256


def draw_strong_index(key, part):
    key = jax.random.fold_in(key, 5)
    blocks = RANGE // RNG_DEV
    keys = jax.random.split(key, blocks)
    picks = jax.vmap(lambda single: jax.random.permutation(single, RNG_DEV)[:STRONG_DEV])(keys)
    offsets = jnp.arange(blocks, dtype=jnp.int32) * RNG_DEV
    return (picks.astype(jnp.int32) + offsets[:, None]).reshape(-1).astype(jnp.int32)


def with_ends(array, key, least, top_value):
    longest = array.shape.index(max(array.shape))
    spots = []
    for shift in (0, 1):
        where = [jax.random.randint(jax.random.fold_in(key, axis), (), 0, length) for axis, length in enumerate(array.shape)]
        where[longest] = (where[longest] + shift) % array.shape[longest]
        spots.append(tuple(where))
    return array.at[spots[0]].set(least).at[spots[1]].set(top_value)


def block_levels(rng, extent, cuts, low, top_value):
    def one(axis_at, parts):
        draws = jax.random.uniform(jax.random.fold_in(jax.random.fold_in(rng, 6), axis_at), (parts,), jnp.float32, low / len(cuts), top_value / len(cuts))
        return jnp.repeat(jnp.exp(draws), extent[axis_at] // parts).reshape((-1,) + (1,) * (len(extent) - axis_at - 1))

    loudness = one(*cuts[0])
    for cut in cuts[1:]:
        loudness = loudness * one(*cut)
    return loudness


def gaussian(own_key, dims, spread, limit, shards=(), held_as=jnp.bfloat16):
    level = block_levels(own_key, dims, shards, -0.22, 0.18) if shards else 1.0
    result = jax.random.normal(own_key, dims, jnp.float32) * spread * level
    return jnp.minimum(jnp.maximum(result, -limit), limit).astype(held_as)


def setup_inputs(seed: int = 0) -> dict:
    key_of = jax.random.split(jax.random.key(seed), 5)
    sar_image = gaussian(key_of[0], (2, RANGE, PULSES), 1.0, 6.0, ((1, 8), (2, 4)), jnp.float32)
    strong_index = draw_strong_index(jax.random.fold_in(key_of[4], 71), 0)
    shifts = with_ends(jax.random.randint(key_of[2], (STRONG_TOTAL,), 0, PULSES), jax.random.fold_in(key_of[2], 1), 0, PULSES - 1).astype(jnp.int32)
    widths = with_ends(jax.random.randint(key_of[3], (STRONG_TOTAL,), PULSES // 64, PULSES // 8 + 1), jax.random.fold_in(key_of[3], 1), PULSES // 64, (PULSES // 8 + 1) - 1).astype(jnp.int32)
    return dict(sar_image=sar_image, strong_index=strong_index, shifts=shifts, widths=widths)


epsilon = 1e-6


def reference(sar_image, strong_index, shifts, widths):
    pulses = sar_image.shape[2]
    field = sar_image[0] + 1j * sar_image[1]
    history = jnp.fft.fft(field, axis=1, norm="ortho")
    cells = jnp.arange(pulses, dtype=jnp.int32)
    source = (cells[None, :] + shifts[:, None] - pulses // 2) % pulses
    lower = pulses // 2 - widths // 2
    window = (cells[None, :] >= lower[:, None]) & (cells[None, :] < (lower + widths)[:, None])
    total = jnp.zeros((pulses,), jnp.float32)
    for step in range(ITERS):
        if step == 0:
            current = field[strong_index]
        else:
            current = jnp.fft.ifft(history[strong_index] * jnp.exp(-1j * total)[None, :], axis=1, norm="ortho")
        centered = jnp.take_along_axis(current, source, axis=1) * window
        spectra = jnp.fft.fft(centered, axis=1, norm="ortho")
        cross = jnp.sum(jnp.imag(jnp.conj(spectra[:, :-1]) * spectra[:, 1:]), axis=0)
        numerator = jnp.concatenate([jnp.zeros((1,), cross.dtype), cross])
        denominator = jnp.sum(jnp.real(spectra) ** 2 + jnp.imag(spectra) ** 2, axis=0)
        total = total + jnp.cumsum(numerator / (denominator + epsilon))
    final = jnp.fft.ifft(history * jnp.exp(-1j * total)[None, :], axis=1, norm="ortho")
    focused_image = jnp.stack([jnp.real(final), jnp.imag(final)]).astype(jnp.float32)
    return focused_image, total.astype(jnp.float32)
```

```python
import functools
import math

import jax
import jax.numpy as jnp
import ml_dtypes
import numpy as np
from jax import lax
from jax.experimental import pallas as pl
from jax.experimental.pallas import tpu as pltpu
from jax.sharding import PartitionSpec as P

ITERS = 2
SIDE = 128
MESH = pl.DeviceIdType.MESH

epsilon = 1e-06


def split(value):
    high = value.astype(ml_dtypes.bfloat16)
    low = (value - high.astype(np.float64)).astype(ml_dtypes.bfloat16)
    return high, low


def make_tables():
    pulses = SIDE * SIDE
    grid = np.arange(SIDE)[:, None] * np.arange(SIDE)[None, :]
    angle = 2.0 * math.pi / SIDE * (grid % SIDE)
    cosine, sine = np.cos(angle), np.sin(angle)
    ahead = np.block([[cosine, sine], [-sine, cosine]])
    back = np.block([[cosine, -sine], [sine, cosine]])
    ahead_h, ahead_l = split(ahead)
    back_h, back_l = split(back)
    turn = 2.0 * math.pi / pulses * grid
    twist = np.stack([np.tile(np.cos(turn), (1, 2)), np.tile(np.sin(turn), (1, 2))]) / SIDE
    return (
        np.concatenate([ahead_h, ahead_l, ahead_h], axis=1),
        np.concatenate([back_h, back_h, back_l], axis=0),
        np.concatenate([ahead_h, ahead_h, ahead_l], axis=0),
        np.concatenate([back_h, back_l, back_h], axis=1),
        twist.astype(np.float32),
    )


def make_turns():
    units = np.arange(SIDE)
    coarse = 2.0 * math.pi / SIDE * units
    fine = 2.0 * math.pi / (SIDE * SIDE) * units
    columns = []
    for exact in (-np.cos(coarse), -np.sin(coarse), np.cos(fine), np.sin(fine)):
        high = np.round(exact * 2048.0) / 2048.0
        columns += [high, exact - high]
    return np.concatenate(columns).astype(np.float32)


def line_turn(turns, shift):
    coarse, fine = shift // SIDE, shift % SIDE
    cc_h, cc_l, cs_h, cs_l = [turns[coarse + SIDE * at] for at in range(4)]
    fc_h, fc_l, fs_h, fs_l = [turns[fine + SIDE * at] for at in range(4, 8)]
    cos_h = cc_h * fc_h - cs_h * fs_h
    cos_l = (cc_h * fc_l + cc_l * (fc_h + fc_l)) - (cs_h * fs_l + cs_l * (fs_h + fs_l))
    sin_h = cs_h * fc_h + cc_h * fs_h
    sin_l = (cs_h * fc_l + cs_l * (fc_h + fc_l)) + (cc_h * fs_l + cc_l * (fs_h + fs_l))
    return cos_h, cos_l, sin_h, sin_l


def halves(value):
    high = value.astype(jnp.bfloat16)
    low = (value - high.astype(jnp.float32)).astype(jnp.bfloat16)
    return high, low


def left(matrix_ref, value):
    high, low = halves(value)
    stacked = jnp.concatenate([high, high, low], axis=0)
    return jnp.dot(matrix_ref[...], stacked, preferred_element_type=jnp.float32)


def right(value, matrix_ref):
    high, low = halves(value)
    stacked = jnp.concatenate([high, low, high], axis=1)
    return jnp.dot(stacked, matrix_ref[...], preferred_element_type=jnp.float32)


def lanes_to_rows(real_part, imag_part):
    return jnp.concatenate(
        [
            jnp.concatenate([real_part[:, :SIDE], imag_part[:, :SIDE]], axis=1),
            jnp.concatenate([real_part[:, SIDE:], imag_part[:, SIDE:]], axis=1),
        ],
        axis=0,
    )


def rows_to_lanes(value):
    real_part = jnp.concatenate([value[:SIDE, :SIDE], value[SIDE:, :SIDE]], axis=1)
    imag_part = jnp.concatenate([value[:SIDE, SIDE:], value[SIDE:, SIDE:]], axis=1)
    return real_part, imag_part


def forward(pair, ahead_left, back_right, twist):
    section = left(ahead_left, pair)
    sec_r, sec_i = section[:SIDE], section[SIDE:]
    cosine, sine = twist[0], twist[1]
    turned = lanes_to_rows(sec_r * cosine + sec_i * sine, sec_i * cosine - sec_r * sine)
    return right(turned, back_right)


def inverse(spectrum, ahead_right, back_left, twist):
    sec_r, sec_i = rows_to_lanes(right(spectrum, ahead_right))
    cosine, sine = twist[0], twist[1]
    turned = jnp.concatenate(
        [sec_r * cosine - sec_i * sine, sec_i * cosine + sec_r * sine], axis=0
    )
    return left(back_left, turned)


def correct(spectrum, cosine, sine):
    rows = []
    for line in range(2):
        part = spectrum[line * SIDE : (line + 1) * SIDE]
        real_part, imag_part = part[:, :SIDE], part[:, SIDE:]
        rows.append(
            jnp.concatenate(
                [real_part * cosine + imag_part * sine, imag_part * cosine - real_part * sine],
                axis=1,
            )
        )
    return jnp.concatenate(rows, axis=0)


def previous(value):
    down = pltpu.roll(value, 1, 0)
    top = down[:8]
    wrapped = pltpu.roll(top, 1, 1)
    first = lax.broadcasted_iota(jnp.int32, (8, SIDE), 0) == 0
    return jnp.concatenate([jnp.where(first, wrapped, top), down[8:]], axis=0)


def kernel(
    ranks,
    parts,
    strong,
    sar_hbm,
    places,
    turns,
    ahead_left_hbm,
    back_right_hbm,
    ahead_right_hbm,
    back_left_hbm,
    twist_hbm,
    image_hbm,
    phase_out,
    sar,
    ahead_left,
    back_right,
    ahead_right,
    back_left,
    twist,
    plain,
    stage,
    rows,
    hist,
    sums,
    phase,
    sums_out,
    sums_in,
    grads,
    ready,
    landed,
    image,
    load_sem,
    image_sem,
    in_send,
    in_recv,
    sum_send,
    sum_recv,
    grad_send,
    grad_recv,
    out_send,
    out_recv,
):
    devices = ranks * parts
    reducers = sums_out.shape[1]
    block = SIDE // reducers
    rank = lax.axis_index("rng")
    part = lax.axis_index("az")
    me = rank * parts + part
    lines = rows.shape[1]
    pairs = lines // 2
    bins = stage.shape[1]
    depth = stage.shape[2]
    mine_strong = strong // parts
    mine_other = lines - mine_strong
    strong_pairs = mine_strong // 2
    groups = bins // 8
    slot_at, bin_at, shift_at, width_at = 0, bins, 2 * bins, 2 * bins + strong

    loads = [
        pltpu.make_async_copy(source, target, load_sem.at[at])
        for at, (source, target) in enumerate(
            [
                (sar_hbm, sar),
                (ahead_left_hbm, ahead_left),
                (twist_hbm, twist),
                (back_right_hbm, back_right),
                (ahead_right_hbm, ahead_right),
                (back_left_hbm, back_left),
            ]
        )
    ]
    loads[0].start()

    barrier = pltpu.get_barrier_semaphore()

    @pl.loop(1, devices)
    def _(step):
        other = (me + step) % devices
        pl.semaphore_signal(
            barrier, inc=1, device_id=(other // parts, other % parts), device_id_type=MESH
        )

    for load in loads[1:]:
        load.start()
    loads[0].wait()

    for half in range(2):

        @pl.loop(0, groups)
        def _(group):
            spot = pl.ds(pl.multiple_of(group * 8, 8), 8)
            plain[half, spot] = sar[half, spot, :].reshape(8, depth, SIDE)

    def arrange(first, last):
        @pl.loop(first, last)
        def _(slot):
            source = places[bin_at + slot]
            for half in range(2):
                stage[half, slot] = plain[half, source]

    arrange(0, strong)
    pl.semaphore_wait(barrier, devices - 1)

    mine = pl.ds(pl.multiple_of(part * depth, depth), depth)

    def strong_slot(pair, owner):
        return mine_strong * owner + 2 * pair

    def other_slot(pair, owner):
        return strong + mine_other * owner + 2 * (pair - strong_pairs)

    def bring(slot_of, pair, source, target):
        return pltpu.make_async_remote_copy(
            src_ref=stage.at[:, pl.ds(slot_of(pair, target), 2)],
            dst_ref=rows.at[:, pl.ds(2 * pair, 2), pl.ds(pl.multiple_of(source * depth, depth), depth)],
            send_sem=in_send.at[pair, target],
            recv_sem=in_recv.at[pair, source],
            device_id=(rank, target),
            device_id_type=MESH,
        )

    order = sorted(range(1, parts), key=lambda step: abs(step - parts // 2))

    def begin(slot_of, pair):
        for step in order:
            bring(slot_of, pair, part, (part + step) % parts).start()

    def arrived(slot_of, pair):
        for step in order:
            other = (part + step) % parts
            bring(slot_of, pair, other, other).wait_recv()

    @pl.loop(0, strong_pairs)
    def _(pair):
        begin(strong_slot, pair)

    arrange(strong, bins)
    for half in range(2):

        @pl.loop(0, mine_strong)
        def _(line):
            rows[half, line, mine, :] = stage[half, mine_strong * part + line]

        @pl.loop(0, mine_other)
        def _(line):
            rows[half, mine_strong + line, mine, :] = stage[half, strong + mine_other * part + line]

    sums[...] = jnp.zeros_like(sums)
    cells = (
        lax.broadcasted_iota(jnp.int32, (SIDE, SIDE), 0) * SIDE
        + lax.broadcasted_iota(jnp.int32, (SIDE, SIDE), 1)
    )
    for load in loads[1:]:
        load.wait()

    def add_terms(pair, value):
        masks = []
        for line in range(2):
            at = mine_strong * part + pair * 2 + line
            width = places[width_at + at]
            offset = (cells - (places[shift_at + at] - width // 2)) & (SIDE * SIDE - 1)
            masks.append((offset < width).astype(jnp.float32))
        mask = jnp.concatenate(masks, axis=1)
        mask = jnp.concatenate([mask, mask], axis=0)
        spectra = forward(value * mask, ahead_left, back_right, twist)
        num = sums[0]
        den = sums[1]
        for line in range(2):
            at = mine_strong * part + pair * 2 + line
            cos_h, cos_l, sin_h, sin_l = line_turn(turns, places[shift_at + at])
            spec_r = spectra[line * SIDE : (line + 1) * SIDE, :SIDE]
            spec_i = spectra[line * SIDE : (line + 1) * SIDE, SIDE:]
            prev_r, prev_i = previous(spec_r), previous(spec_i)
            cross_i = prev_r * spec_i - prev_i * spec_r
            cross_r = prev_r * spec_r + prev_i * spec_i
            rest = cross_i * cos_l + cross_r * sin_l
            num = num + ((cross_i * cos_h + cross_r * sin_h) + rest)
            den = den + (spec_r * spec_r + spec_i * spec_i)
        sums[0] = num
        sums[1] = den

    def gathered(pair):
        return jnp.concatenate(
            [
                jnp.concatenate([rows[half, pair * 2], rows[half, pair * 2 + 1]], axis=1)
                for half in range(2)
            ],
            axis=0,
        )

    @pl.loop(0, strong_pairs)
    def _(pair):
        arrived(strong_slot, pair)
        if pairs == 2 * strong_pairs:
            begin(other_slot, strong_pairs + pair)
        value = gathered(pair)
        hist[pair] = forward(value, ahead_left, back_right, twist)
        add_terms(pair, value)

    if pairs != 2 * strong_pairs:

        @pl.loop(strong_pairs, pairs)
        def _(pair):
            begin(other_slot, pair)

    def rest_of_history(first, last):
        @pl.loop(first, last)
        def _(pair):
            arrived(other_slot, pair)
            hist[pair] = forward(gathered(pair), ahead_left, back_right, twist)

    eight_rows = lax.broadcasted_iota(jnp.int32, (8, SIDE), 0)
    row_ids = lax.broadcasted_iota(jnp.int32, (SIDE, SIDE), 0)
    col_ids = lax.broadcasted_iota(jnp.int32, (SIDE, SIDE), 1)

    def reduce_sums(turn, before, after):
        for owner in range(reducers):
            sums_out[turn, owner, :block, :] = sums[0, owner * block : (owner + 1) * block, :]
            sums_out[turn, owner, block:, :] = sums[1, owner * block : (owner + 1) * block, :]

        def give(source, target):
            return pltpu.make_async_remote_copy(
                src_ref=sums_out.at[turn, target],
                dst_ref=sums_in.at[turn, source],
                send_sem=sum_send.at[turn, target],
                recv_sem=sum_recv.at[turn, source],
                device_id=(target // parts, target % parts),
                device_id_type=MESH,
            )

        def share(source, target):
            return pltpu.make_async_remote_copy(
                src_ref=grads.at[turn, source],
                dst_ref=grads.at[turn, source],
                send_sem=grad_send.at[turn, target],
                recv_sem=grad_recv.at[turn, source],
                device_id=(target // parts, target % parts),
                device_id_type=MESH,
            )

        def each_other(count, act):
            if count == devices:

                @pl.loop(1, devices)
                def _(step):
                    act((me + step) % devices)

            else:

                @pl.loop(0, count)
                def _(other):
                    @pl.when(other != me)
                    def _():
                        act(other)

        def reducing(act):
            if reducers == devices:
                act()
            else:
                pl.when(me < reducers)(act)

        each_other(reducers, lambda other: give(me, other).start())

        before()

        def combine():
            def add(step, total):
                other = (me + step) % devices
                give(other, me).wait_recv()
                return total + sums_in[turn, other]

            total = lax.fori_loop(1, devices, add, sums_out[turn, me])
            swapped = pltpu.roll(total, block, 0)
            upper = eight_rows < block
            num = jnp.where(upper, total, swapped)
            den = jnp.where(upper, swapped, total)
            no_first = (
                (eight_rows % block == 0)
                & (lax.broadcasted_iota(jnp.int32, (8, SIDE), 1) == 0)
                & (me == 0)
            )
            grads[turn, me] = jnp.where(no_first, 0.0, num / (den + epsilon))
            each_other(devices, lambda other: share(me, other).start())

        reducing(combine)
        after()
        each_other(reducers, lambda other: share(other, other).wait_recv())
        tiles = [
            jnp.where(eight_rows < block, grads[turn, 2 * at], grads[turn, 2 * at + 1])
            for at in range(reducers // 2)
        ]
        gradient = jnp.concatenate(tiles, axis=0)
        lower = (row_ids >= col_ids).astype(jnp.float32)
        upper = (row_ids < col_ids).astype(jnp.float32)
        inside = jnp.dot(
            lower, gradient, precision=lax.Precision.HIGHEST, preferred_element_type=jnp.float32
        )
        columns = jnp.broadcast_to(inside[SIDE - 1 :], (8, SIDE))
        before = jnp.dot(
            columns, upper, precision=lax.Precision.HIGHEST, preferred_element_type=jnp.float32
        )
        running = inside + before[:1]
        phase[...] = running if turn == 0 else phase[...] + running
        each_other(reducers, lambda other: give(me, other).wait_send())

        def drain():
            each_other(devices, lambda other: share(me, other).wait_send())

        reducing(drain)

    def nothing():
        pass

    halfway = strong_pairs + (pairs - strong_pairs) // 2
    reduce_sums(0, nothing, nothing)
    for turn in range(1, ITERS):
        cosine, sine = jnp.cos(phase[...]), jnp.sin(phase[...])
        sums[...] = jnp.zeros_like(sums)

        @pl.loop(0, strong_pairs)
        def _(pair):
            add_terms(
                pair, inverse(correct(hist[pair], cosine, sine), ahead_right, back_left, twist)
            )

        if turn == ITERS - 1:
            reduce_sums(
                turn,
                lambda: rest_of_history(strong_pairs, halfway),
                lambda: rest_of_history(halfway, pairs),
            )
        else:
            reduce_sums(turn, nothing, nothing)

    cosine, sine = jnp.cos(phase[...]), jnp.sin(phase[...])

    def send_out(slot_of, pair, source, target):
        return pltpu.make_async_remote_copy(
            src_ref=ready.at[:, pl.ds(2 * pair, 2), pl.ds(pl.multiple_of(target * depth, depth), depth)],
            dst_ref=landed.at[:, pl.ds(slot_of(pair, source), 2)],
            send_sem=out_send.at[pair, target],
            recv_sem=out_recv.at[pair, source],
            device_id=(rank, target),
            device_id_type=MESH,
        )

    kinds = ((0, strong_pairs, strong_slot), (strong_pairs, pairs, other_slot))
    for first, last, slot_of in kinds:

        @pl.loop(first, last)
        def _(pair):
            value = inverse(correct(hist[pair], cosine, sine), ahead_right, back_left, twist)
            for half in range(2):
                for line in range(2):
                    ready[half, 2 * pair + line] = value[
                        half * SIDE : (half + 1) * SIDE, line * SIDE : (line + 1) * SIDE
                    ]
            for step in order:
                send_out(slot_of, pair, part, (part + step) % parts).start()
            for half in range(2):
                for line in range(2):
                    landed[half, slot_of(pair, part) + line] = ready[half, 2 * pair + line, mine, :]

    plain[0, : SIDE // depth] = phase[...].T.reshape(SIDE // depth, depth, SIDE)
    phase_out[...] = plain[0, part]

    for first, last, slot_of in kinds:

        @pl.loop(first, last)
        def _(pair):
            for step in order:
                bring(slot_of, pair, part, (part + step) % parts).wait_send()
            for step in order:
                other = (part + step) % parts
                send_out(slot_of, pair, other, other).wait_recv()

    def write(half, group):
        spot = pl.ds(pl.multiple_of(group * 8, 8), 8)
        return pltpu.make_async_copy(
            image.at[half, spot], image_hbm.at[half, spot], image_sem.at[half, group]
        )

    for half in range(2):

        @pl.loop(0, groups)
        def _(group):
            found = [landed[half, places[slot_at + group * 8 + at]] for at in range(8)]
            spot = pl.ds(pl.multiple_of(group * 8, 8), 8)
            image[half, spot, :] = jnp.stack(found).reshape(8, depth * SIDE)
            write(half, group).start()

    for first, last, slot_of in kinds:

        @pl.loop(first, last)
        def _(pair):
            for step in order:
                send_out(slot_of, pair, part, (part + step) % parts).wait_send()

    for half in range(2):

        @pl.loop(0, groups)
        def _(group):
            write(half, group).wait()


def local(ranks, parts, sar_image, strong_index, shifts, widths):
    bins = sar_image.shape[1]
    here = sar_image.shape[2]
    depth = here // SIDE
    lines = bins // parts
    pairs = lines // 2
    strong = strong_index.shape[0]
    devices = ranks * parts
    reducers = min(devices, SIDE // 4)
    chosen = strong_index % bins
    ids = jnp.arange(bins, dtype=jnp.int32)
    same = chosen[None, :] == ids[:, None]
    ahead = (chosen[None, :] < ids[:, None]).astype(jnp.int32)
    order = jnp.arange(strong, dtype=jnp.int32)[None, :]
    is_strong = jnp.any(same, axis=1)
    slots = jnp.where(
        is_strong,
        jnp.sum(jnp.where(same, order, 0), axis=1),
        strong + ids - jnp.sum(ahead, axis=1),
    )
    located = jnp.sum(jnp.where(slots[None, :] == ids[:, None], ids[None, :], 0), axis=1)
    places = jnp.concatenate([slots, located, shifts, widths])
    tables = make_tables()
    vmem = pl.BlockSpec(memory_space=pltpu.VMEM)
    smem = pl.BlockSpec(memory_space=pltpu.SMEM)
    anywhere = pl.BlockSpec(memory_space=pl.ANY)
    dma = pltpu.SemaphoreType.DMA
    image, phase = pl.pallas_call(
        functools.partial(kernel, ranks, parts, strong),
        out_shape=(
            jax.ShapeDtypeStruct((2, bins, here), jnp.float32),
            jax.ShapeDtypeStruct((depth, SIDE), jnp.float32),
        ),
        in_specs=[anywhere, smem, smem] + [anywhere] * 5,
        out_specs=(anywhere, vmem),
        scratch_shapes=[
            pltpu.VMEM((2, bins, here), jnp.float32),
            pltpu.VMEM(tables[0].shape, jnp.bfloat16),
            pltpu.VMEM(tables[1].shape, jnp.bfloat16),
            pltpu.VMEM(tables[2].shape, jnp.bfloat16),
            pltpu.VMEM(tables[3].shape, jnp.bfloat16),
            pltpu.VMEM(tables[4].shape, jnp.float32),
            pltpu.VMEM((2, bins, depth, SIDE), jnp.float32),
            pltpu.VMEM((2, bins, depth, SIDE), jnp.float32),
            pltpu.VMEM((2, lines, SIDE, SIDE), jnp.float32),
            pltpu.VMEM((pairs, 2 * SIDE, 2 * SIDE), jnp.float32),
            pltpu.VMEM((2, SIDE, SIDE), jnp.float32),
            pltpu.VMEM((SIDE, SIDE), jnp.float32),
            pltpu.VMEM((ITERS, reducers, 8, SIDE), jnp.float32),
            pltpu.VMEM((ITERS, devices, 8, SIDE), jnp.float32),
            pltpu.VMEM((ITERS, reducers, 8, SIDE), jnp.float32),
            pltpu.VMEM((2, lines, SIDE, SIDE), jnp.float32),
            pltpu.VMEM((2, bins, depth, SIDE), jnp.float32),
            pltpu.VMEM((2, bins, here), jnp.float32),
            dma((6,)),
            dma((2, bins // 8)),
            dma((pairs, parts)),
            dma((pairs, parts)),
            dma((ITERS, reducers)),
            dma((ITERS, devices)),
            dma((ITERS, devices)),
            dma((ITERS, reducers)),
            dma((pairs, parts)),
            dma((pairs, parts)),
        ],
        compiler_params=pltpu.CompilerParams(
            collective_id=0, has_side_effects=True, vmem_limit_bytes=40 * 2**20
        ),
        name="autofocus",
    )(sar_image, places, jnp.asarray(make_turns()), *[jnp.asarray(t) for t in tables])
    return image, phase.reshape(here)


def solution(mesh):
    placed = (P(None, "rng", "az"), P("rng"), P("rng"), P("rng"))
    return jax.shard_map(
        functools.partial(local, mesh.shape["rng"], mesh.shape["az"]),
        mesh=mesh,
        in_specs=placed,
        out_specs=(P(None, "rng", "az"), P("az")),
        check_vma=False,
    )
```

```python
import functools
import math

import jax
import jax.numpy as jnp
import numpy as np
from jax import lax
from jax.experimental import pallas as pl
from jax.experimental.pallas import tpu as pltpu
from jax.sharding import PartitionSpec as P

ITERS = 2
SIDE = 128
MESH = pl.DeviceIdType.MESH

epsilon = 1e-06


def make_tables(unit):
    pulses = SIDE * SIDE
    grid = np.arange(SIDE)[:, None] * np.arange(SIDE)[None, :]
    angle = 2.0 * math.pi / SIDE * (grid % SIDE)
    cosine, sine = np.cos(angle), np.sin(angle)
    ahead = np.block([[cosine, sine], [-sine, cosine]])
    back = np.block([[cosine, -sine], [sine, cosine]])
    turn = 2.0 * math.pi / pulses * grid
    twist = np.stack([np.tile(np.cos(turn), (1, unit)), np.tile(np.sin(turn), (1, unit))]) / SIDE
    return np.stack([ahead, back]).astype(np.float32), twist.astype(np.float32)


def make_turns():
    units = np.arange(SIDE)
    coarse = 2.0 * math.pi / SIDE * units
    fine = 2.0 * math.pi / (SIDE * SIDE) * units
    columns = []
    for exact in (-np.cos(coarse), -np.sin(coarse), np.cos(fine), np.sin(fine)):
        high = np.round(exact * 2048.0) / 2048.0
        columns += [high, exact - high]
    return np.concatenate(columns).astype(np.float32)


def line_turn(turns, shift):
    coarse, fine = shift // SIDE, shift % SIDE
    cc_h, cc_l, cs_h, cs_l = [turns[coarse + SIDE * at] for at in range(4)]
    fc_h, fc_l, fs_h, fs_l = [turns[fine + SIDE * at] for at in range(4, 8)]
    cos_h = cc_h * fc_h - cs_h * fs_h
    cos_l = (cc_h * fc_l + cc_l * (fc_h + fc_l)) - (cs_h * fs_l + cs_l * (fs_h + fs_l))
    sin_h = cs_h * fc_h + cc_h * fs_h
    sin_l = (cs_h * fc_l + cs_l * (fc_h + fc_l)) + (cc_h * fs_l + cc_l * (fs_h + fs_l))
    return cos_h, cos_l, sin_h, sin_l


def halves(value):
    high = value.astype(jnp.bfloat16)
    low = (value - high.astype(jnp.float32)).astype(jnp.bfloat16)
    return high, low


def left(matrix_ref, value):
    high, low = halves(value)
    stacked = jnp.concatenate([high, high, low], axis=0)
    return jnp.dot(matrix_ref[...], stacked, preferred_element_type=jnp.float32)


def right(value, matrix_ref):
    high, low = halves(value)
    stacked = jnp.concatenate([high, low, high], axis=1)
    return jnp.dot(stacked, matrix_ref[...], preferred_element_type=jnp.float32)


def lanes_to_rows(real_part, imag_part):
    lines = real_part.shape[1] // SIDE
    spots = [slice(line * SIDE, (line + 1) * SIDE) for line in range(lines)]
    return jnp.concatenate(
        [jnp.concatenate([real_part[:, at], imag_part[:, at]], axis=1) for at in spots], axis=0
    )


def rows_to_lanes(value):
    lines = value.shape[0] // SIDE
    spots = [slice(line * SIDE, (line + 1) * SIDE) for line in range(lines)]
    real_part = jnp.concatenate([value[at, :SIDE] for at in spots], axis=1)
    imag_part = jnp.concatenate([value[at, SIDE:] for at in spots], axis=1)
    return real_part, imag_part


def forward(pair, ahead_left, back_right, twist):
    section = left(ahead_left, pair)
    sec_r, sec_i = section[:SIDE], section[SIDE:]
    cosine, sine = twist[0], twist[1]
    turned = lanes_to_rows(sec_r * cosine + sec_i * sine, sec_i * cosine - sec_r * sine)
    return right(turned, back_right)


def inverse(spectrum, ahead_right, back_left, twist):
    sec_r, sec_i = rows_to_lanes(right(spectrum, ahead_right))
    cosine, sine = twist[0], twist[1]
    turned = jnp.concatenate(
        [sec_r * cosine - sec_i * sine, sec_i * cosine + sec_r * sine], axis=0
    )
    return left(back_left, turned)


def correct(spectrum, cosine, sine):
    rows = []
    for line in range(spectrum.shape[0] // SIDE):
        part = spectrum[line * SIDE : (line + 1) * SIDE]
        real_part, imag_part = part[:, :SIDE], part[:, SIDE:]
        rows.append(
            jnp.concatenate(
                [real_part * cosine + imag_part * sine, imag_part * cosine - real_part * sine],
                axis=1,
            )
        )
    return jnp.concatenate(rows, axis=0)


def previous(value):
    down = pltpu.roll(value, 1, 0)
    top = down[:8]
    wrapped = pltpu.roll(top, 1, 1)
    first = lax.broadcasted_iota(jnp.int32, (8, SIDE), 0) == 0
    return jnp.concatenate([jnp.where(first, wrapped, top), down[8:]], axis=0)


def kernel(
    ranks,
    parts,
    strong,
    sar_hbm,
    places,
    turns,
    matrices_hbm,
    twist_hbm,
    image_hbm,
    phase_out,
    sar,
    matrices,
    ahead_left,
    back_right,
    ahead_right,
    back_left,
    twist,
    plain,
    stage,
    rows,
    hist,
    sums,
    phase,
    near_in,
    far_in,
    grads,
    ready,
    landed,
    image,
    load_sem,
    image_sem,
    in_send,
    in_recv,
    near_send,
    near_recv,
    far_send,
    far_recv,
    grad_send,
    grad_recv,
    out_send,
    out_recv,
):
    devices = ranks * parts
    near = near_in.shape[1]
    far = far_in.shape[1]
    block = SIDE // near
    rank = lax.axis_index("rng")
    part = lax.axis_index("az")
    me = rank * parts + part
    lines = rows.shape[1]
    units = hist.shape[0]
    unit = lines // units
    bins = stage.shape[1]
    depth = stage.shape[2]
    mine_strong = strong // parts
    mine_other = lines - mine_strong
    strong_units = mine_strong // unit
    groups = bins // 8
    slot_at, bin_at, shift_at, width_at = 0, bins, 2 * bins, 2 * bins + strong

    loads = [
        pltpu.make_async_copy(source, target, load_sem.at[at])
        for at, (source, target) in enumerate(
            [
                (sar_hbm, sar),
                (matrices_hbm, matrices),
                (twist_hbm, twist),
            ]
        )
    ]
    loads[0].start()

    barrier = pltpu.get_barrier_semaphore()

    def at_device(other):
        return (other // parts, other % parts)

    group_near, place_near = me // near, me % near

    def near_device(place):
        return group_near * near + place

    def far_device(group):
        return group * near + place_near

    greeted = [near_device((place_near + step) % near) for step in range(1, near)]
    if far <= 8:
        greeted += [far_device((group_near + step) % far) for step in range(1, far)]
    if parts > near or near % parts:
        greeted += [rank * parts + (part + step) % parts for step in range(1, parts)]
    for other in greeted:
        pl.semaphore_signal(barrier, inc=1, device_id=at_device(other), device_id_type=MESH)
    awaited = len(greeted)
    if far > 8:
        awaited += far - 1

        @pl.loop(1, far)
        def _(step):
            other = far_device((group_near + step) % far)
            pl.semaphore_signal(barrier, inc=1, device_id=at_device(other), device_id_type=MESH)

    for load in loads[1:]:
        load.start()
    loads[0].wait()

    for half in range(2):

        @pl.loop(0, groups)
        def _(group):
            spot = pl.ds(pl.multiple_of(group * 8, 8), 8)
            plain[half, spot] = sar[half, spot, :].reshape(8, depth, SIDE)

    def arrange(first, last):
        @pl.loop(first, last)
        def _(slot):
            source = places[bin_at + slot]
            for half in range(2):
                stage[half, slot] = plain[half, source]

    arrange(0, strong)
    pl.semaphore_wait(barrier, awaited)

    mine = pl.ds(pl.multiple_of(part * depth, depth), depth)

    def strong_slot(pair, owner):
        return mine_strong * owner + unit * pair

    def other_slot(pair, owner):
        return strong + mine_other * owner + unit * (pair - strong_units)

    def bring(slot_of, pair, source, target):
        return pltpu.make_async_remote_copy(
            src_ref=stage.at[:, pl.ds(slot_of(pair, target), unit)],
            dst_ref=rows.at[:, pl.ds(unit * pair, unit), pl.ds(pl.multiple_of(source * depth, depth), depth)],
            send_sem=in_send.at[pair, target],
            recv_sem=in_recv.at[pair, source],
            device_id=(rank, target),
            device_id_type=MESH,
        )

    order = sorted(range(1, parts), key=lambda step: abs(step - parts // 2))

    def begin(slot_of, pair):
        for step in order:
            bring(slot_of, pair, part, (part + step) % parts).start()

    def arrived(slot_of, pair):
        for step in order:
            other = (part + step) % parts
            bring(slot_of, pair, other, other).wait_recv()

    @pl.loop(0, strong_units)
    def _(pair):
        begin(strong_slot, pair)

    arrange(strong, bins)
    for half in range(2):

        @pl.loop(0, mine_strong)
        def _(line):
            rows[half, line, mine, :] = stage[half, mine_strong * part + line]

        @pl.loop(0, mine_other)
        def _(line):
            rows[half, mine_strong + line, mine, :] = stage[half, strong + mine_other * part + line]

    sums[...] = jnp.zeros_like(sums)
    cells = (
        lax.broadcasted_iota(jnp.int32, (SIDE, SIDE), 0) * SIDE
        + lax.broadcasted_iota(jnp.int32, (SIDE, SIDE), 1)
    )
    for load in loads[1:]:
        load.wait()
    ahead_h, ahead_l = halves(matrices[0])
    back_h, back_l = halves(matrices[1])
    ahead_left[...] = jnp.concatenate([ahead_h, ahead_l, ahead_h], axis=1)
    back_right[...] = jnp.concatenate([back_h, back_h, back_l], axis=0)
    ahead_right[...] = jnp.concatenate([ahead_h, ahead_h, ahead_l], axis=0)
    back_left[...] = jnp.concatenate([back_h, back_l, back_h], axis=1)

    def add_terms(turn, pair, value):
        masks = []
        for line in range(unit):
            at = mine_strong * part + pair * unit + line
            width = places[width_at + at]
            offset = (cells - (places[shift_at + at] - width // 2)) & (SIDE * SIDE - 1)
            masks.append((offset < width).astype(jnp.float32))
        mask = jnp.concatenate(masks, axis=1)
        mask = jnp.concatenate([mask, mask], axis=0)
        spectra = forward(value * mask, ahead_left, back_right, twist)
        num = sums[turn, 0]
        den = sums[turn, 1]
        for line in range(unit):
            at = mine_strong * part + pair * unit + line
            cos_h, cos_l, sin_h, sin_l = line_turn(turns, places[shift_at + at])
            spec_r = spectra[line * SIDE : (line + 1) * SIDE, :SIDE]
            spec_i = spectra[line * SIDE : (line + 1) * SIDE, SIDE:]
            prev_r, prev_i = previous(spec_r), previous(spec_i)
            cross_i = prev_r * spec_i - prev_i * spec_r
            cross_r = prev_r * spec_r + prev_i * spec_i
            rest = cross_i * cos_l + cross_r * sin_l
            num = num + ((cross_i * cos_h + cross_r * sin_h) + rest)
            den = den + (spec_r * spec_r + spec_i * spec_i)
        sums[turn, 0] = num
        sums[turn, 1] = den

    def gathered(pair):
        return jnp.concatenate(
            [
                jnp.concatenate([rows[half, pair * unit + at] for at in range(unit)], axis=1)
                for half in range(2)
            ],
            axis=0,
        )

    @pl.loop(0, strong_units)
    def _(pair):
        arrived(strong_slot, pair)
        if units == 2 * strong_units:
            begin(other_slot, strong_units + pair)
        add_terms(0, pair, gathered(pair))

    if units != 2 * strong_units:

        @pl.loop(strong_units, units)
        def _(pair):
            begin(other_slot, pair)

    def add_history(first, last, slot_of=None):
        @pl.loop(first, last)
        def _(pair):
            if slot_of is not None:
                arrived(slot_of, pair)
            hist[pair] = forward(gathered(pair), ahead_left, back_right, twist)

    row_ids = lax.broadcasted_iota(jnp.int32, (SIDE, SIDE), 0)
    col_ids = lax.broadcasted_iota(jnp.int32, (SIDE, SIDE), 1)
    block_rows = lax.broadcasted_iota(jnp.int32, (block, SIDE), 0)
    block_cols = lax.broadcasted_iota(jnp.int32, (block, SIDE), 1)

    def near_spot(place):
        return pl.ds(pl.multiple_of(place * block, block), block)

    def give(turn, source, target):
        return pltpu.make_async_remote_copy(
            src_ref=sums.at[turn, :, near_spot(target)],
            dst_ref=near_in.at[turn, source],
            send_sem=near_send.at[turn, target],
            recv_sem=near_recv.at[turn, source],
            device_id=at_device(near_device(target)),
            device_id_type=MESH,
        )

    def spread(turn, source, target):
        return pltpu.make_async_remote_copy(
            src_ref=far_in.at[turn, source],
            dst_ref=far_in.at[turn, source],
            send_sem=far_send.at[turn, target],
            recv_sem=far_recv.at[turn, source],
            device_id=at_device(far_device(target)),
            device_id_type=MESH,
        )

    def share(turn, source, target):
        return pltpu.make_async_remote_copy(
            src_ref=grads.at[turn, near_spot(source)],
            dst_ref=grads.at[turn, near_spot(source)],
            send_sem=grad_send.at[turn, target],
            recv_sem=grad_recv.at[turn, source],
            device_id=at_device(near_device(target)),
            device_id_type=MESH,
        )

    def others(own, count, act):
        if count <= 8:
            for step in range(1, count):
                act((own + step) % count)
        else:

            @pl.loop(1, count)
            def _(step):
                act((own + step) % count)

    def reduce_sums(turn, first_task, second_task):
        others(place_near, near, lambda place: give(turn, place_near, place).start())
        first_task()
        total = sums[turn, :, near_spot(place_near), :]
        for step in range(1, near):
            place = (place_near + step) % near
            give(turn, place, place).wait_recv()
            total = total + near_in[turn, place]
        far_in[turn, group_near] = total
        others(group_near, far, lambda group: spread(turn, group_near, group).start())
        second_task()
        others(group_near, far, lambda group: spread(turn, group, group).wait_recv())
        total = far_in[turn, 0]
        if far <= 8:
            for group in range(1, far):
                total = total + far_in[turn, group]
        else:
            total = lax.fori_loop(1, far, lambda group, value: value + far_in[turn, group], total)
        no_first = (block_rows == 0) & (block_cols == 0) & (place_near == 0)
        grads[turn, near_spot(place_near), :] = jnp.where(
            no_first, 0.0, total[0] / (total[1] + epsilon)
        )
        others(place_near, near, lambda place: share(turn, place_near, place).start())
        others(place_near, near, lambda place: share(turn, place, place).wait_recv())
        gradient = grads[turn]
        lower = (row_ids >= col_ids).astype(jnp.float32)
        upper = (row_ids < col_ids).astype(jnp.float32)
        inside = jnp.dot(
            lower, gradient, precision=lax.Precision.HIGHEST, preferred_element_type=jnp.float32
        )
        columns = jnp.broadcast_to(inside[SIDE - 1 :], (8, SIDE))
        before = jnp.dot(
            columns, upper, precision=lax.Precision.HIGHEST, preferred_element_type=jnp.float32
        )
        running = inside + before[:1]
        phase[...] = running if turn == 0 else phase[...] + running

    def drain(turn):
        others(place_near, near, lambda place: give(turn, place_near, place).wait_send())
        others(group_near, far, lambda group: spread(turn, group_near, group).wait_send())
        others(place_near, near, lambda place: share(turn, place_near, place).wait_send())

    def nothing():
        pass

    middle = strong_units // 2
    halfway = strong_units + (units - strong_units) // 2
    for turn in range(ITERS):
        if turn > 0:
            cosine, sine = jnp.cos(phase[...]), jnp.sin(phase[...])

            @pl.loop(0, strong_units)
            def _(pair):
                value = inverse(correct(hist[pair], cosine, sine), ahead_right, back_left, twist)
                add_terms(turn, pair, value)

        first_task, second_task = nothing, nothing
        if turn == 0:
            first_task = lambda: add_history(0, middle)
            second_task = lambda: add_history(middle, strong_units)
        elif turn == ITERS - 1:
            first_task = lambda: add_history(strong_units, halfway, other_slot)
            second_task = lambda: add_history(halfway, units, other_slot)
        reduce_sums(turn, first_task, second_task)

    cosine, sine = jnp.cos(phase[...]), jnp.sin(phase[...])

    def send_out(slot_of, pair, source, target):
        return pltpu.make_async_remote_copy(
            src_ref=ready.at[:, pl.ds(unit * pair, unit), pl.ds(pl.multiple_of(target * depth, depth), depth)],
            dst_ref=landed.at[:, pl.ds(slot_of(pair, source), unit)],
            send_sem=out_send.at[pair, target],
            recv_sem=out_recv.at[pair, source],
            device_id=(rank, target),
            device_id_type=MESH,
        )

    kinds = ((0, strong_units, strong_slot), (strong_units, units, other_slot))
    for first, last, slot_of in kinds:

        @pl.loop(first, last)
        def _(pair):
            value = inverse(correct(hist[pair], cosine, sine), ahead_right, back_left, twist)
            for half in range(2):
                for line in range(unit):
                    ready[half, unit * pair + line] = value[
                        half * SIDE : (half + 1) * SIDE, line * SIDE : (line + 1) * SIDE
                    ]
            for step in order:
                send_out(slot_of, pair, part, (part + step) % parts).start()
            for half in range(2):
                for line in range(unit):
                    landed[half, slot_of(pair, part) + line] = ready[
                        half, unit * pair + line, mine, :
                    ]

    for turn in range(ITERS):
        drain(turn)
    plain[0, : SIDE // depth] = phase[...].T.reshape(SIDE // depth, depth, SIDE)
    phase_out[...] = plain[0, part]

    for first, last, slot_of in kinds:

        @pl.loop(first, last)
        def _(pair):
            for step in order:
                bring(slot_of, pair, part, (part + step) % parts).wait_send()
            for step in order:
                other = (part + step) % parts
                send_out(slot_of, pair, other, other).wait_recv()

    def write(half, group):
        spot = pl.ds(pl.multiple_of(group * 8, 8), 8)
        return pltpu.make_async_copy(
            image.at[half, spot], image_hbm.at[half, spot], image_sem.at[half, group]
        )

    for half in range(2):

        @pl.loop(0, groups)
        def _(group):
            found = [landed[half, places[slot_at + group * 8 + at]] for at in range(8)]
            spot = pl.ds(pl.multiple_of(group * 8, 8), 8)
            image[half, spot, :] = jnp.stack(found).reshape(8, depth * SIDE)
            write(half, group).start()

    for first, last, slot_of in kinds:

        @pl.loop(first, last)
        def _(pair):
            for step in order:
                send_out(slot_of, pair, part, (part + step) % parts).wait_send()

    for half in range(2):

        @pl.loop(0, groups)
        def _(group):
            write(half, group).wait()


def local(ranks, parts, sar_image, strong_index, shifts, widths):
    bins = sar_image.shape[1]
    here = sar_image.shape[2]
    depth = here // SIDE
    lines = bins // parts
    strong = strong_index.shape[0]
    devices = ranks * parts
    unit = min(4, strong // parts)
    units = lines // unit
    near = 8
    far = devices // near
    chosen = strong_index % bins
    ids = jnp.arange(bins, dtype=jnp.int32)
    same = chosen[None, :] == ids[:, None]
    ahead = (chosen[None, :] < ids[:, None]).astype(jnp.int32)
    order = jnp.arange(strong, dtype=jnp.int32)[None, :]
    is_strong = jnp.any(same, axis=1)
    slots = jnp.where(
        is_strong,
        jnp.sum(jnp.where(same, order, 0), axis=1),
        strong + ids - jnp.sum(ahead, axis=1),
    )
    located = jnp.sum(jnp.where(slots[None, :] == ids[:, None], ids[None, :], 0), axis=1)
    places = jnp.concatenate([slots, located, shifts, widths])
    tables = make_tables(unit)
    vmem = pl.BlockSpec(memory_space=pltpu.VMEM)
    smem = pl.BlockSpec(memory_space=pltpu.SMEM)
    anywhere = pl.BlockSpec(memory_space=pltpu.HBM)
    dma = pltpu.SemaphoreType.DMA
    image, phase = pl.pallas_call(
        functools.partial(kernel, ranks, parts, strong),
        out_shape=(
            jax.ShapeDtypeStruct((2, bins, here), jnp.float32),
            jax.ShapeDtypeStruct((depth, SIDE), jnp.float32),
        ),
        in_specs=[anywhere, smem, smem] + [anywhere] * 2,
        out_specs=(anywhere, vmem),
        scratch_shapes=[
            pltpu.VMEM((2, bins, here), jnp.float32),
            pltpu.VMEM(tables[0].shape, jnp.float32),
            pltpu.VMEM((2 * SIDE, 6 * SIDE), jnp.bfloat16),
            pltpu.VMEM((6 * SIDE, 2 * SIDE), jnp.bfloat16),
            pltpu.VMEM((6 * SIDE, 2 * SIDE), jnp.bfloat16),
            pltpu.VMEM((2 * SIDE, 6 * SIDE), jnp.bfloat16),
            pltpu.VMEM(tables[1].shape, jnp.float32),
            pltpu.VMEM((2, bins, depth, SIDE), jnp.float32),
            pltpu.VMEM((2, bins, depth, SIDE), jnp.float32),
            pltpu.VMEM((2, lines, SIDE, SIDE), jnp.float32),
            pltpu.VMEM((units, unit * SIDE, 2 * SIDE), jnp.float32),
            pltpu.VMEM((ITERS, 2, SIDE, SIDE), jnp.float32),
            pltpu.VMEM((SIDE, SIDE), jnp.float32),
            pltpu.VMEM((ITERS, near, 2, SIDE // near, SIDE), jnp.float32),
            pltpu.VMEM((ITERS, far, 2, SIDE // near, SIDE), jnp.float32),
            pltpu.VMEM((ITERS, SIDE, SIDE), jnp.float32),
            pltpu.VMEM((2, lines, SIDE, SIDE), jnp.float32),
            pltpu.VMEM((2, bins, depth, SIDE), jnp.float32),
            pltpu.VMEM((2, bins, here), jnp.float32),
            dma((3,)),
            dma((2, bins // 8)),
            dma((units, parts)),
            dma((units, parts)),
            dma((ITERS, near)),
            dma((ITERS, near)),
            dma((ITERS, far)),
            dma((ITERS, far)),
            dma((ITERS, near)),
            dma((ITERS, near)),
            dma((units, parts)),
            dma((units, parts)),
        ],
        compiler_params=pltpu.CompilerParams(
            collective_id=0, has_side_effects=True, vmem_limit_bytes=56 * 2**20
        ),
        name="autofocus",
    )(sar_image, places, jnp.asarray(make_turns()), *[jnp.asarray(t) for t in tables])
    return image, phase.reshape(here)


def solution(mesh):
    placed = (P(None, "rng", "az"), P("rng"), P("rng"), P("rng"))
    return jax.shard_map(
        functools.partial(local, mesh.shape["rng"], mesh.shape["az"]),
        mesh=mesh,
        in_specs=placed,
        out_specs=(P(None, "rng", "az"), P("az")),
        check_vma=False,
    )
```

```python
import functools
import math

import jax
import jax.numpy as jnp
import numpy as np
from jax import lax
from jax.experimental import pallas as pl
from jax.experimental.pallas import tpu as pltpu
from jax.sharding import PartitionSpec as P

ITERS = 2
SIDE = 128
MESH = pl.DeviceIdType.MESH

epsilon = 1e-06


def make_tables(unit):
    pulses = SIDE * SIDE
    grid = np.arange(SIDE)[:, None] * np.arange(SIDE)[None, :]
    angle = 2.0 * math.pi / SIDE * (grid % SIDE)
    cosine, sine = np.cos(angle), np.sin(angle)
    ahead = np.block([[cosine, sine], [-sine, cosine]])
    back = np.block([[cosine, -sine], [sine, cosine]])
    turn = 2.0 * math.pi / pulses * grid
    twist = np.stack([np.tile(np.cos(turn), (1, unit)), np.tile(np.sin(turn), (1, unit))]) / SIDE
    return np.stack([ahead, back]).astype(np.float32), twist.astype(np.float32)


def make_turns():
    units = np.arange(SIDE)
    coarse = 2.0 * math.pi / SIDE * units
    fine = 2.0 * math.pi / (SIDE * SIDE) * units
    columns = []
    for exact in (-np.cos(coarse), -np.sin(coarse), np.cos(fine), np.sin(fine)):
        high = np.round(exact * 2048.0) / 2048.0
        columns += [high, exact - high]
    return np.concatenate(columns).astype(np.float32)


def line_turn(turns, shift):
    coarse, fine = shift // SIDE, shift % SIDE
    cc_h, cc_l, cs_h, cs_l = [turns[coarse + SIDE * at] for at in range(4)]
    fc_h, fc_l, fs_h, fs_l = [turns[fine + SIDE * at] for at in range(4, 8)]
    cos_h = cc_h * fc_h - cs_h * fs_h
    cos_l = (cc_h * fc_l + cc_l * (fc_h + fc_l)) - (cs_h * fs_l + cs_l * (fs_h + fs_l))
    sin_h = cs_h * fc_h + cc_h * fs_h
    sin_l = (cs_h * fc_l + cs_l * (fc_h + fc_l)) + (cc_h * fs_l + cc_l * (fs_h + fs_l))
    return cos_h, cos_l, sin_h, sin_l


def halves(value):
    high = value.astype(jnp.bfloat16)
    low = (value - high.astype(jnp.float32)).astype(jnp.bfloat16)
    return high, low


def left(matrix_ref, value):
    high, low = halves(value)
    stacked = jnp.concatenate([high, high, low], axis=0)
    return jnp.dot(matrix_ref[...], stacked, preferred_element_type=jnp.float32)


def right(value, matrix_ref):
    high, low = halves(value)
    stacked = jnp.concatenate([high, low, high], axis=1)
    return jnp.dot(stacked, matrix_ref[...], preferred_element_type=jnp.float32)


def lanes_to_rows(real_part, imag_part):
    lines = real_part.shape[1] // SIDE
    spots = [slice(line * SIDE, (line + 1) * SIDE) for line in range(lines)]
    return jnp.concatenate(
        [jnp.concatenate([real_part[:, at], imag_part[:, at]], axis=1) for at in spots], axis=0
    )


def rows_to_lanes(value):
    lines = value.shape[0] // SIDE
    spots = [slice(line * SIDE, (line + 1) * SIDE) for line in range(lines)]
    real_part = jnp.concatenate([value[at, :SIDE] for at in spots], axis=1)
    imag_part = jnp.concatenate([value[at, SIDE:] for at in spots], axis=1)
    return real_part, imag_part


def forward(pair, ahead_left, back_right, twist):
    section = left(ahead_left, pair)
    sec_r, sec_i = section[:SIDE], section[SIDE:]
    cosine, sine = twist[0], twist[1]
    turned = lanes_to_rows(sec_r * cosine + sec_i * sine, sec_i * cosine - sec_r * sine)
    return right(turned, back_right)


def inverse(spectrum, ahead_right, back_left, twist):
    sec_r, sec_i = rows_to_lanes(right(spectrum, ahead_right))
    cosine, sine = twist[0], twist[1]
    turned = jnp.concatenate(
        [sec_r * cosine - sec_i * sine, sec_i * cosine + sec_r * sine], axis=0
    )
    return left(back_left, turned)


def correct(spectrum, cosine, sine):
    rows = []
    for line in range(spectrum.shape[0] // SIDE):
        part = spectrum[line * SIDE : (line + 1) * SIDE]
        real_part, imag_part = part[:, :SIDE], part[:, SIDE:]
        rows.append(
            jnp.concatenate(
                [real_part * cosine + imag_part * sine, imag_part * cosine - real_part * sine],
                axis=1,
            )
        )
    return jnp.concatenate(rows, axis=0)


def previous(value):
    down = pltpu.roll(value, 1, 0)
    top = down[:8]
    wrapped = pltpu.roll(top, 1, 1)
    first = lax.broadcasted_iota(jnp.int32, (8, SIDE), 0) == 0
    return jnp.concatenate([jnp.where(first, wrapped, top), down[8:]], axis=0)


def kernel(
    ranks,
    parts,
    strong,
    sar_hbm,
    places,
    turns,
    matrices_hbm,
    twist_hbm,
    landed,
    phase_out,
    sar,
    matrices,
    ahead_left,
    back_right,
    ahead_right,
    back_left,
    twist,
    plain,
    natural,
    stage,
    rows,
    hist,
    sums,
    phase,
    near_in,
    far_in,
    grads,
    ready,
    load_sem,
    own_sem,
    in_send,
    in_recv,
    near_send,
    near_recv,
    far_send,
    far_recv,
    grad_send,
    grad_recv,
    out_send,
    out_recv,
):
    devices = ranks * parts
    near = near_in.shape[1]
    far = far_in.shape[1]
    block = SIDE // near
    rank = lax.axis_index("rng")
    part = lax.axis_index("az")
    me = rank * parts + part
    lines = rows.shape[1]
    units = hist.shape[0]
    unit = lines // units
    bins = stage.shape[1]
    depth = stage.shape[2]
    mine_strong = strong // parts
    mine_other = lines - mine_strong
    strong_units = mine_strong // unit
    groups = bins // 8
    slot_at, bin_at, shift_at, width_at = 0, bins, 2 * bins, 2 * bins + strong

    loads = [
        pltpu.make_async_copy(source, target, load_sem.at[at])
        for at, (source, target) in enumerate(
            [
                (sar_hbm, sar),
                (matrices_hbm, matrices),
                (twist_hbm, twist),
            ]
        )
    ]
    loads[0].start()

    barrier = pltpu.get_barrier_semaphore()

    def at_device(other):
        return (other // parts, other % parts)

    group_near, place_near = me // near, me % near

    def near_device(place):
        return group_near * near + place

    def far_device(group):
        return group * near + place_near

    greeted = [near_device((place_near + step) % near) for step in range(1, near)]
    if far <= 8:
        greeted += [far_device((group_near + step) % far) for step in range(1, far)]
    if parts > near or near % parts:
        greeted += [rank * parts + (part + step) % parts for step in range(1, parts)]
    for other in greeted:
        pl.semaphore_signal(barrier, inc=1, device_id=at_device(other), device_id_type=MESH)
    awaited = len(greeted)
    if far > 8:
        awaited += far - 1

        @pl.loop(1, far)
        def _(step):
            other = far_device((group_near + step) % far)
            pl.semaphore_signal(barrier, inc=1, device_id=at_device(other), device_id_type=MESH)

    for load in loads[1:]:
        load.start()
    loads[0].wait()

    for half in range(2):

        @pl.loop(0, groups)
        def _(group):
            spot = pl.ds(pl.multiple_of(group * 8, 8), 8)
            for cut in range(depth):
                plain[pl.ds((half * bins + group * 8) * depth + cut, 8, stride=depth), :] = sar[
                    half, spot, cut * SIDE : (cut + 1) * SIDE
                ]
            for at in range(8):
                start = pl.multiple_of((half * bins + group * 8 + at) * depth, depth)
                natural[half, group * 8 + at] = plain[pl.ds(start, depth), :]

    def arrange(first, last):
        @pl.loop(first, last)
        def _(slot):
            source = places[bin_at + slot]
            for half in range(2):
                stage[half, slot] = natural[half, source]

    arrange(0, strong)
    pl.semaphore_wait(barrier, awaited)

    mine = pl.ds(pl.multiple_of(part * depth, depth), depth)

    def strong_slot(pair, owner):
        return mine_strong * owner + unit * pair

    def other_slot(pair, owner):
        return strong + mine_other * owner + unit * (pair - strong_units)

    def bring(slot_of, pair, source, target):
        return pltpu.make_async_remote_copy(
            src_ref=stage.at[:, pl.ds(slot_of(pair, target), unit)],
            dst_ref=rows.at[:, pl.ds(unit * pair, unit), pl.ds(pl.multiple_of(source * depth, depth), depth)],
            send_sem=in_send.at[pair, target],
            recv_sem=in_recv.at[pair, source],
            device_id=(rank, target),
            device_id_type=MESH,
        )

    order = sorted(range(1, parts), key=lambda step: abs(step - parts // 2))

    def begin(slot_of, pair):
        for step in order:
            bring(slot_of, pair, part, (part + step) % parts).start()

    def arrived(slot_of, pair):
        for step in order:
            other = (part + step) % parts
            bring(slot_of, pair, other, other).wait_recv()

    @pl.loop(0, strong_units)
    def _(pair):
        begin(strong_slot, pair)

    arrange(strong, bins)
    for half in range(2):

        @pl.loop(0, mine_strong)
        def _(line):
            rows[half, line, mine, :] = stage[half, mine_strong * part + line]

        @pl.loop(0, mine_other)
        def _(line):
            rows[half, mine_strong + line, mine, :] = stage[half, strong + mine_other * part + line]

    sums[...] = jnp.zeros_like(sums)
    cells = (
        lax.broadcasted_iota(jnp.int32, (SIDE, SIDE), 0) * SIDE
        + lax.broadcasted_iota(jnp.int32, (SIDE, SIDE), 1)
    )
    for load in loads[1:]:
        load.wait()
    ahead_h, ahead_l = halves(matrices[0])
    back_h, back_l = halves(matrices[1])
    ahead_left[...] = jnp.concatenate([ahead_h, ahead_l, ahead_h], axis=1)
    back_right[...] = jnp.concatenate([back_h, back_h, back_l], axis=0)
    ahead_right[...] = jnp.concatenate([ahead_h, ahead_h, ahead_l], axis=0)
    back_left[...] = jnp.concatenate([back_h, back_l, back_h], axis=1)

    def add_terms(turn, pair, value):
        masks = []
        for line in range(unit):
            at = mine_strong * part + pair * unit + line
            width = places[width_at + at]
            offset = (cells - (places[shift_at + at] - width // 2)) & (SIDE * SIDE - 1)
            masks.append((offset < width).astype(jnp.float32))
        mask = jnp.concatenate(masks, axis=1)
        mask = jnp.concatenate([mask, mask], axis=0)
        spectra = forward(value * mask, ahead_left, back_right, twist)
        num = sums[turn, 0]
        den = sums[turn, 1]
        for line in range(unit):
            at = mine_strong * part + pair * unit + line
            cos_h, cos_l, sin_h, sin_l = line_turn(turns, places[shift_at + at])
            spec_r = spectra[line * SIDE : (line + 1) * SIDE, :SIDE]
            spec_i = spectra[line * SIDE : (line + 1) * SIDE, SIDE:]
            prev_r, prev_i = previous(spec_r), previous(spec_i)
            cross_i = prev_r * spec_i - prev_i * spec_r
            cross_r = prev_r * spec_r + prev_i * spec_i
            rest = cross_i * cos_l + cross_r * sin_l
            num = num + ((cross_i * cos_h + cross_r * sin_h) + rest)
            den = den + (spec_r * spec_r + spec_i * spec_i)
        sums[turn, 0] = num
        sums[turn, 1] = den

    def gathered(pair):
        return jnp.concatenate(
            [
                jnp.concatenate([rows[half, pair * unit + at] for at in range(unit)], axis=1)
                for half in range(2)
            ],
            axis=0,
        )

    @pl.loop(0, strong_units)
    def _(pair):
        arrived(strong_slot, pair)
        if units == 2 * strong_units:
            begin(other_slot, strong_units + pair)
        add_terms(0, pair, gathered(pair))

    if units != 2 * strong_units:

        @pl.loop(strong_units, units)
        def _(pair):
            begin(other_slot, pair)

    def add_history(first, last, slot_of=None):
        @pl.loop(first, last)
        def _(pair):
            if slot_of is not None:
                arrived(slot_of, pair)
            hist[pair] = forward(gathered(pair), ahead_left, back_right, twist)

    row_ids = lax.broadcasted_iota(jnp.int32, (SIDE, SIDE), 0)
    col_ids = lax.broadcasted_iota(jnp.int32, (SIDE, SIDE), 1)
    block_rows = lax.broadcasted_iota(jnp.int32, (block, SIDE), 0)
    block_cols = lax.broadcasted_iota(jnp.int32, (block, SIDE), 1)

    def near_spot(place):
        return pl.ds(pl.multiple_of(place * block, block), block)

    def give(turn, source, target):
        return pltpu.make_async_remote_copy(
            src_ref=sums.at[turn, :, near_spot(target)],
            dst_ref=near_in.at[turn, source],
            send_sem=near_send.at[turn, target],
            recv_sem=near_recv.at[turn, source],
            device_id=at_device(near_device(target)),
            device_id_type=MESH,
        )

    def spread(turn, source, target):
        return pltpu.make_async_remote_copy(
            src_ref=far_in.at[turn, source],
            dst_ref=far_in.at[turn, source],
            send_sem=far_send.at[turn, target],
            recv_sem=far_recv.at[turn, source],
            device_id=at_device(far_device(target)),
            device_id_type=MESH,
        )

    def share(turn, source, target):
        return pltpu.make_async_remote_copy(
            src_ref=grads.at[turn, near_spot(source)],
            dst_ref=grads.at[turn, near_spot(source)],
            send_sem=grad_send.at[turn, target],
            recv_sem=grad_recv.at[turn, source],
            device_id=at_device(near_device(target)),
            device_id_type=MESH,
        )

    def others(own, count, act):
        if count <= 8:
            for step in range(1, count):
                act((own + step) % count)
        else:

            @pl.loop(1, count)
            def _(step):
                act((own + step) % count)

    def reduce_sums(turn, first_task, second_task):
        others(place_near, near, lambda place: give(turn, place_near, place).start())
        first_task()
        total = sums[turn, :, near_spot(place_near), :]
        for step in range(1, near):
            place = (place_near + step) % near
            give(turn, place, place).wait_recv()
            total = total + near_in[turn, place]
        far_in[turn, group_near] = total
        others(group_near, far, lambda group: spread(turn, group_near, group).start())
        second_task()
        others(group_near, far, lambda group: spread(turn, group, group).wait_recv())
        total = far_in[turn, 0]
        if far <= 8:
            for group in range(1, far):
                total = total + far_in[turn, group]
        else:
            total = lax.fori_loop(1, far, lambda group, value: value + far_in[turn, group], total)
        no_first = (block_rows == 0) & (block_cols == 0) & (place_near == 0)
        grads[turn, near_spot(place_near), :] = jnp.where(
            no_first, 0.0, total[0] / (total[1] + epsilon)
        )
        others(place_near, near, lambda place: share(turn, place_near, place).start())
        others(place_near, near, lambda place: share(turn, place, place).wait_recv())
        gradient = grads[turn]
        lower = (row_ids >= col_ids).astype(jnp.float32)
        upper = (row_ids < col_ids).astype(jnp.float32)
        inside = jnp.dot(
            lower, gradient, precision=lax.Precision.HIGHEST, preferred_element_type=jnp.float32
        )
        columns = jnp.broadcast_to(inside[SIDE - 1 :], (8, SIDE))
        before = jnp.dot(
            columns, upper, precision=lax.Precision.HIGHEST, preferred_element_type=jnp.float32
        )
        running = inside + before[:1]
        phase[...] = running if turn == 0 else phase[...] + running

    def drain(turn):
        others(place_near, near, lambda place: give(turn, place_near, place).wait_send())
        others(group_near, far, lambda group: spread(turn, group_near, group).wait_send())
        others(place_near, near, lambda place: share(turn, place_near, place).wait_send())

    def nothing():
        pass

    middle = strong_units // 2
    halfway = strong_units + (units - strong_units) // 2
    for turn in range(ITERS):
        if turn > 0:
            cosine, sine = jnp.cos(phase[...]), jnp.sin(phase[...])

            @pl.loop(0, strong_units)
            def _(pair):
                value = inverse(correct(hist[pair], cosine, sine), ahead_right, back_left, twist)
                add_terms(turn, pair, value)

        first_task, second_task = nothing, nothing
        if turn == 0:
            first_task = lambda: add_history(0, middle)
            second_task = lambda: add_history(middle, strong_units)
        elif turn == ITERS - 1:
            first_task = lambda: add_history(strong_units, halfway, other_slot)
            second_task = lambda: add_history(halfway, units, other_slot)
        reduce_sums(turn, first_task, second_task)

    cosine, sine = jnp.cos(phase[...]), jnp.sin(phase[...])

    def send_out(slot_of, pair, source, target):
        return pltpu.make_async_remote_copy(
            src_ref=ready.at[:, pl.ds(unit * pair, unit), pl.ds(pl.multiple_of(target * depth, depth), depth)],
            dst_ref=landed.at[:, pl.ds(slot_of(pair, source), unit)],
            send_sem=out_send.at[pair, target],
            recv_sem=out_recv.at[pair, source],
            device_id=(rank, target),
            device_id_type=MESH,
        )

    def keep(slot_of, pair):
        return pltpu.make_async_copy(
            ready.at[:, pl.ds(unit * pair, unit), mine],
            landed.at[:, pl.ds(slot_of(pair, part), unit)],
            own_sem.at[pair],
        )

    kinds = ((0, strong_units, strong_slot), (strong_units, units, other_slot))
    for first, last, slot_of in kinds:

        @pl.loop(first, last)
        def _(pair):
            value = inverse(correct(hist[pair], cosine, sine), ahead_right, back_left, twist)
            for half in range(2):
                for line in range(unit):
                    ready[half, unit * pair + line] = value[
                        half * SIDE : (half + 1) * SIDE, line * SIDE : (line + 1) * SIDE
                    ]
            for step in order:
                send_out(slot_of, pair, part, (part + step) % parts).start()
            keep(slot_of, pair).start()

    for turn in range(ITERS):
        drain(turn)
    turned = phase[...].T
    plain[:SIDE, :] = turned
    phase_out[...] = plain[mine, :]

    for first, last, slot_of in kinds:

        @pl.loop(first, last)
        def _(pair):
            for step in order:
                bring(slot_of, pair, part, (part + step) % parts).wait_send()
            for step in order:
                other = (part + step) % parts
                send_out(slot_of, pair, other, other).wait_recv()
                send_out(slot_of, pair, part, other).wait_send()
            keep(slot_of, pair).wait()

def place_rows(
    landed_hbm, places, phase, image_hbm, phase_out, landed, plain, image, load_sem, image_sem
):
    bins = landed.shape[1]
    depth = landed.shape[2]
    groups = bins // 8
    loads = [
        pltpu.make_async_copy(landed_hbm.at[half], landed.at[half], load_sem.at[half])
        for half in range(2)
    ]
    for load in loads:
        load.start()
    phase_out[...] = phase[...]

    def write(half, group):
        spot = pl.ds(pl.multiple_of(group * 8, 8), 8)
        return pltpu.make_async_copy(
            image.at[half, spot], image_hbm.at[half, spot], image_sem.at[half, group]
        )

    for half in range(2):
        loads[half].wait()

        @pl.loop(0, groups)
        def _(group):
            base = (half * bins + group * 8) * depth
            for at in range(8):
                plain[pl.ds(pl.multiple_of(base + at * depth, depth), depth), :] = landed[
                    half, places[group * 8 + at]
                ]
            spot = pl.ds(pl.multiple_of(group * 8, 8), 8)
            for cut in range(depth):
                image[half, spot, cut * SIDE : (cut + 1) * SIDE] = plain[
                    pl.ds(base + cut, 8, stride=depth), :
                ]
            write(half, group).start()

    for half in range(2):

        @pl.loop(0, groups)
        def _(group):
            write(half, group).wait()


def local(ranks, parts, sar_image, strong_index, shifts, widths):
    bins = sar_image.shape[1]
    here = sar_image.shape[2]
    depth = here // SIDE
    lines = bins // parts
    strong = strong_index.shape[0]
    devices = ranks * parts
    unit = min(4, strong // parts)
    units = lines // unit
    near = 8
    far = devices // near
    chosen = strong_index % bins
    ids = jnp.arange(bins, dtype=jnp.int32)
    same = chosen[None, :] == ids[:, None]
    ahead = (chosen[None, :] < ids[:, None]).astype(jnp.int32)
    order = jnp.arange(strong, dtype=jnp.int32)[None, :]
    is_strong = jnp.any(same, axis=1)
    slots = jnp.where(
        is_strong,
        jnp.sum(jnp.where(same, order, 0), axis=1),
        strong + ids - jnp.sum(ahead, axis=1),
    )
    located = jnp.sum(jnp.where(slots[None, :] == ids[:, None], ids[None, :], 0), axis=1)
    places = jnp.concatenate([slots, located, shifts, widths])
    tables = make_tables(unit)
    vmem = pl.BlockSpec(memory_space=pltpu.VMEM)
    smem = pl.BlockSpec(memory_space=pltpu.SMEM)
    anywhere = pl.BlockSpec(memory_space=pltpu.HBM)
    dma = pltpu.SemaphoreType.DMA
    landed, phase = pl.pallas_call(
        functools.partial(kernel, ranks, parts, strong),
        out_shape=(
            jax.ShapeDtypeStruct((2, bins, depth, SIDE), jnp.float32),
            jax.ShapeDtypeStruct((depth, SIDE), jnp.float32),
        ),
        in_specs=[anywhere, smem, smem] + [anywhere] * 2,
        out_specs=(anywhere, vmem),
        scratch_shapes=[
            pltpu.VMEM((2, bins, here), jnp.float32),
            pltpu.VMEM(tables[0].shape, jnp.float32),
            pltpu.VMEM((2 * SIDE, 6 * SIDE), jnp.bfloat16),
            pltpu.VMEM((6 * SIDE, 2 * SIDE), jnp.bfloat16),
            pltpu.VMEM((6 * SIDE, 2 * SIDE), jnp.bfloat16),
            pltpu.VMEM((2 * SIDE, 6 * SIDE), jnp.bfloat16),
            pltpu.VMEM(tables[1].shape, jnp.float32),
            pltpu.VMEM((2 * bins * depth, SIDE), jnp.float32),
            pltpu.VMEM((2, bins, depth, SIDE), jnp.float32),
            pltpu.VMEM((2, bins, depth, SIDE), jnp.float32),
            pltpu.VMEM((2, lines, SIDE, SIDE), jnp.float32),
            pltpu.VMEM((units, unit * SIDE, 2 * SIDE), jnp.float32),
            pltpu.VMEM((ITERS, 2, SIDE, SIDE), jnp.float32),
            pltpu.VMEM((SIDE, SIDE), jnp.float32),
            pltpu.VMEM((ITERS, near, 2, SIDE // near, SIDE), jnp.float32),
            pltpu.VMEM((ITERS, far, 2, SIDE // near, SIDE), jnp.float32),
            pltpu.VMEM((ITERS, SIDE, SIDE), jnp.float32),
            pltpu.VMEM((2, lines, SIDE, SIDE), jnp.float32),
            dma((3,)),
            dma((units,)),
            dma((units, parts)),
            dma((units, parts)),
            dma((ITERS, near)),
            dma((ITERS, near)),
            dma((ITERS, far)),
            dma((ITERS, far)),
            dma((ITERS, near)),
            dma((ITERS, near)),
            dma((units, parts)),
            dma((units, parts)),
        ],
        compiler_params=pltpu.CompilerParams(
            collective_id=0, has_side_effects=True, vmem_limit_bytes=56 * 2**20
        ),
        name="autofocus",
    )(sar_image, places, jnp.asarray(make_turns()), *[jnp.asarray(t) for t in tables])
    image, phase = pl.pallas_call(
        place_rows,
        out_shape=(
            jax.ShapeDtypeStruct((2, bins, here), jnp.float32),
            jax.ShapeDtypeStruct((depth, SIDE), jnp.float32),
        ),
        in_specs=[anywhere, smem, vmem],
        out_specs=(anywhere, vmem),
        scratch_shapes=[
            pltpu.VMEM((2, bins, depth, SIDE), jnp.float32),
            pltpu.VMEM((2 * bins * depth, SIDE), jnp.float32),
            pltpu.VMEM((2, bins, here), jnp.float32),
            dma((2,)),
            dma((2, bins // 8)),
        ],
        compiler_params=pltpu.CompilerParams(vmem_limit_bytes=56 * 2**20),
        name="place_rows",
    )(landed, places, phase)
    return image, phase.reshape(here)


def solution(mesh):
    placed = (P(None, "rng", "az"), P("rng"), P("rng"), P("rng"))
    return jax.shard_map(
        functools.partial(local, mesh.shape["rng"], mesh.shape["az"]),
        mesh=mesh,
        in_specs=placed,
        out_specs=(P(None, "rng", "az"), P("az")),
        check_vma=False,
    )
```

```python
import functools
import math

import jax
import jax.numpy as jnp
import numpy as np
from jax import lax
from jax.experimental import pallas as pl
from jax.experimental.pallas import tpu as pltpu
from jax.sharding import PartitionSpec as P

ITERS = 2
SIDE = 128
MESH = pl.DeviceIdType.MESH

epsilon = 1e-06


def make_tables(unit):
    pulses = SIDE * SIDE
    grid = np.arange(SIDE)[:, None] * np.arange(SIDE)[None, :]
    angle = 2.0 * math.pi / SIDE * (grid % SIDE)
    cosine, sine = np.cos(angle), np.sin(angle)
    ahead = np.block([[cosine, sine], [-sine, cosine]])
    back = np.block([[cosine, -sine], [sine, cosine]])
    turn = 2.0 * math.pi / pulses * grid
    twist = np.stack([np.tile(np.cos(turn), (1, unit)), np.tile(np.sin(turn), (1, unit))]) / SIDE
    return np.stack([ahead, back]).astype(np.float32), twist.astype(np.float32)


def make_turns():
    units = np.arange(SIDE)
    coarse = 2.0 * math.pi / SIDE * units
    fine = 2.0 * math.pi / (SIDE * SIDE) * units
    columns = []
    for exact in (-np.cos(coarse), -np.sin(coarse), np.cos(fine), np.sin(fine)):
        high = np.round(exact * 2048.0) / 2048.0
        columns += [high, exact - high]
    return np.concatenate(columns).astype(np.float32)


def line_turn(turns, shift):
    coarse, fine = shift // SIDE, shift % SIDE
    cc_h, cc_l, cs_h, cs_l = [turns[coarse + SIDE * at] for at in range(4)]
    fc_h, fc_l, fs_h, fs_l = [turns[fine + SIDE * at] for at in range(4, 8)]
    cos_h = cc_h * fc_h - cs_h * fs_h
    cos_l = (cc_h * fc_l + cc_l * (fc_h + fc_l)) - (cs_h * fs_l + cs_l * (fs_h + fs_l))
    sin_h = cs_h * fc_h + cc_h * fs_h
    sin_l = (cs_h * fc_l + cs_l * (fc_h + fc_l)) + (cc_h * fs_l + cc_l * (fs_h + fs_l))
    return cos_h, cos_l, sin_h, sin_l


def halves(value):
    high = value.astype(jnp.bfloat16)
    low = (value - high.astype(jnp.float32)).astype(jnp.bfloat16)
    return high, low


def left(matrix_ref, value):
    high, low = halves(value)
    stacked = jnp.concatenate([high, high, low], axis=0)
    return jnp.dot(matrix_ref[...], stacked, preferred_element_type=jnp.float32)


def right(value, matrix_ref):
    high, low = halves(value)
    stacked = jnp.concatenate([high, low, high], axis=1)
    return jnp.dot(stacked, matrix_ref[...], preferred_element_type=jnp.float32)


def lanes_to_rows(real_part, imag_part):
    lines = real_part.shape[1] // SIDE
    spots = [slice(line * SIDE, (line + 1) * SIDE) for line in range(lines)]
    return jnp.concatenate(
        [jnp.concatenate([real_part[:, at], imag_part[:, at]], axis=1) for at in spots], axis=0
    )


def rows_to_lanes(value):
    lines = value.shape[0] // SIDE
    spots = [slice(line * SIDE, (line + 1) * SIDE) for line in range(lines)]
    real_part = jnp.concatenate([value[at, :SIDE] for at in spots], axis=1)
    imag_part = jnp.concatenate([value[at, SIDE:] for at in spots], axis=1)
    return real_part, imag_part


def forward(pair, ahead_left, back_right, twist):
    section = left(ahead_left, pair)
    sec_r, sec_i = section[:SIDE], section[SIDE:]
    cosine, sine = twist[0], twist[1]
    turned = lanes_to_rows(sec_r * cosine + sec_i * sine, sec_i * cosine - sec_r * sine)
    return right(turned, back_right)


def inverse(spectrum, ahead_right, back_left, twist):
    sec_r, sec_i = rows_to_lanes(right(spectrum, ahead_right))
    cosine, sine = twist[0], twist[1]
    turned = jnp.concatenate(
        [sec_r * cosine - sec_i * sine, sec_i * cosine + sec_r * sine], axis=0
    )
    return left(back_left, turned)


def correct(spectrum, cosine, sine):
    rows = []
    for line in range(spectrum.shape[0] // SIDE):
        part = spectrum[line * SIDE : (line + 1) * SIDE]
        real_part, imag_part = part[:, :SIDE], part[:, SIDE:]
        rows.append(
            jnp.concatenate(
                [real_part * cosine + imag_part * sine, imag_part * cosine - real_part * sine],
                axis=1,
            )
        )
    return jnp.concatenate(rows, axis=0)


def previous(value):
    down = pltpu.roll(value, 1, 0)
    top = down[:8]
    wrapped = pltpu.roll(top, 1, 1)
    first = lax.broadcasted_iota(jnp.int32, (8, SIDE), 0) == 0
    return jnp.concatenate([jnp.where(first, wrapped, top), down[8:]], axis=0)


def kernel(
    ranks,
    parts,
    strong,
    sar_hbm,
    places,
    turns,
    matrices_hbm,
    twist_hbm,
    landed,
    phase_out,
    sar,
    matrices,
    ahead_left,
    back_right,
    ahead_right,
    back_left,
    back_part,
    twist,
    plain,
    natural,
    stage,
    rows,
    hist,
    sums,
    phase,
    near_in,
    far_in,
    grads,
    ready,
    prepared,
    load_sem,
    own_sem,
    in_send,
    in_recv,
    near_send,
    near_recv,
    far_send,
    far_recv,
    grad_send,
    grad_recv,
    out_send,
    out_recv,
    pass_send,
    pass_recv,
):
    devices = ranks * parts
    near = near_in.shape[1]
    far = far_in.shape[1]
    block = SIDE // near
    rank = lax.axis_index("rng")
    part = lax.axis_index("az")
    me = rank * parts + part
    lines = rows.shape[1]
    units = hist.shape[0]
    unit = lines // units
    bins = stage.shape[1]
    depth = stage.shape[2]
    core = part % 2
    twin = part + 1 - 2 * core
    wide = 2 * depth
    mine_strong = strong // parts
    mine_other = lines - mine_strong
    strong_units = mine_strong // unit
    ratio = (units - strong_units) // strong_units
    groups = bins // 8
    slot_at, bin_at, shift_at, width_at = 0, bins, 2 * bins, 2 * bins + strong

    loads = [
        pltpu.make_async_copy(source, target, load_sem.at[at])
        for at, (source, target) in enumerate(
            [
                (sar_hbm, sar),
                (matrices_hbm, matrices),
                (twist_hbm, twist),
            ]
        )
    ]
    loads[0].start()

    barrier = pltpu.get_barrier_semaphore()

    def at_device(other):
        return (other // parts, other % parts)

    group_near, place_near = me // near, me % near

    def near_device(place):
        return group_near * near + place

    def far_device(group):
        return group * near + place_near

    greeted = [near_device((place_near + step) % near) for step in range(1, near)]
    if far <= 8:
        greeted += [far_device((group_near + step) % far) for step in range(1, far)]
    if parts > near or near % parts:
        greeted += [rank * parts + (part + step) % parts for step in range(1, parts)]
    for other in greeted:
        pl.semaphore_signal(barrier, inc=1, device_id=at_device(other), device_id_type=MESH)
    awaited = len(greeted)
    if far > 8:
        awaited += far - 1

        @pl.loop(1, far)
        def _(step):
            other = far_device((group_near + step) % far)
            pl.semaphore_signal(barrier, inc=1, device_id=at_device(other), device_id_type=MESH)

    for load in loads[1:]:
        load.start()
    loads[0].wait()

    for half in range(2):

        @pl.loop(0, groups)
        def _(group):
            spot = pl.ds(pl.multiple_of(group * 8, 8), 8)
            for cut in range(depth):
                plain[pl.ds((half * bins + group * 8) * depth + cut, 8, stride=depth), :] = sar[
                    half, spot, cut * SIDE : (cut + 1) * SIDE
                ]
            for at in range(8):
                start = pl.multiple_of((half * bins + group * 8 + at) * depth, depth)
                natural[half, group * 8 + at] = plain[pl.ds(start, depth), :]

    def arrange(first, last):
        @pl.loop(first, last)
        def _(slot):
            source = places[bin_at + slot]
            for half in range(2):
                stage[half, slot] = natural[half, source]

    arrange(0, strong)
    pl.semaphore_wait(barrier, awaited)

    mine = pl.ds(pl.multiple_of(part * depth, depth), depth)

    def strong_slot(pair, owner):
        return mine_strong * owner + unit * pair

    def other_slot(pair, owner):
        return strong + mine_other * (owner % 2) + unit * (pair - strong_units)

    def bring(slot_of, pair, source, target):
        return pltpu.make_async_remote_copy(
            src_ref=stage.at[:, pl.ds(slot_of(pair, target), unit)],
            dst_ref=rows.at[:, pl.ds(unit * pair, unit), pl.ds(pl.multiple_of(source * depth, depth), depth)],
            send_sem=in_send.at[pair, target],
            recv_sem=in_recv.at[pair, source],
            device_id=(rank, target),
            device_id_type=MESH,
        )

    order = sorted(range(1, parts), key=lambda step: abs(step - parts // 2))

    def begin(slot_of, pair):
        for step in order:
            bring(slot_of, pair, part, (part + step) % parts).start()

    def arrived(slot_of, pair):
        for step in order:
            other = (part + step) % parts
            bring(slot_of, pair, other, other).wait_recv()

    @pl.loop(0, strong_units)
    def _(pair):
        begin(strong_slot, pair)

    arrange(strong, bins)
    for half in range(2):

        @pl.loop(0, mine_strong)
        def _(line):
            rows[half, line, mine, :] = stage[half, mine_strong * part + line]

        @pl.loop(0, mine_other)
        def _(line):
            rows[half, mine_strong + line, mine, :] = stage[half, strong + mine_other * core + line]

    sums[...] = jnp.zeros_like(sums)
    cells = (
        lax.broadcasted_iota(jnp.int32, (SIDE, SIDE), 0) * SIDE
        + lax.broadcasted_iota(jnp.int32, (SIDE, SIDE), 1)
    )
    for load in loads[1:]:
        load.wait()
    ahead_h, ahead_l = halves(matrices[0])
    back_h, back_l = halves(matrices[1])
    ahead_left[...] = jnp.concatenate([ahead_h, ahead_l, ahead_h], axis=1)
    back_right[...] = jnp.concatenate([back_h, back_h, back_l], axis=0)
    ahead_right[...] = jnp.concatenate([ahead_h, ahead_h, ahead_l], axis=0)
    back_left[...] = jnp.concatenate([back_h, back_l, back_h], axis=1)
    half_rows = pl.multiple_of((part // 2) * wide, wide)
    part_h, part_l = halves(
        jnp.concatenate(
            [
                matrices[1, pl.ds(half_rows, wide), :],
                matrices[1, pl.ds(pl.multiple_of(SIDE + half_rows, wide), wide), :],
            ],
            axis=0,
        )
    )
    back_part[...] = jnp.concatenate([part_h, part_l, part_h], axis=1)

    def add_terms(turn, pair, value):
        masks = []
        for line in range(unit):
            at = mine_strong * part + pair * unit + line
            width = places[width_at + at]
            offset = (cells - (places[shift_at + at] - width // 2)) & (SIDE * SIDE - 1)
            masks.append((offset < width).astype(jnp.float32))
        mask = jnp.concatenate(masks, axis=1)
        mask = jnp.concatenate([mask, mask], axis=0)
        spectra = forward(value * mask, ahead_left, back_right, twist)
        num = sums[turn, 0]
        den = sums[turn, 1]
        for line in range(unit):
            at = mine_strong * part + pair * unit + line
            cos_h, cos_l, sin_h, sin_l = line_turn(turns, places[shift_at + at])
            spec_r = spectra[line * SIDE : (line + 1) * SIDE, :SIDE]
            spec_i = spectra[line * SIDE : (line + 1) * SIDE, SIDE:]
            prev_r, prev_i = previous(spec_r), previous(spec_i)
            cross_i = prev_r * spec_i - prev_i * spec_r
            cross_r = prev_r * spec_r + prev_i * spec_i
            rest = cross_i * cos_l + cross_r * sin_l
            num = num + ((cross_i * cos_h + cross_r * sin_h) + rest)
            den = den + (spec_r * spec_r + spec_i * spec_i)
        sums[turn, 0] = num
        sums[turn, 1] = den

    def gathered(pair):
        return jnp.concatenate(
            [
                jnp.concatenate([rows[half, pair * unit + at] for at in range(unit)], axis=1)
                for half in range(2)
            ],
            axis=0,
        )

    @pl.loop(0, strong_units)
    def _(pair):
        arrived(strong_slot, pair)
        for at in range(ratio):
            begin(other_slot, strong_units + pair * ratio + at)
        add_terms(0, pair, gathered(pair))

    def add_history(first, last, slot_of=None):
        @pl.loop(first, last)
        def _(pair):
            if slot_of is not None:
                arrived(slot_of, pair)
            hist[pair] = forward(gathered(pair), ahead_left, back_right, twist)

    row_ids = lax.broadcasted_iota(jnp.int32, (SIDE, SIDE), 0)
    col_ids = lax.broadcasted_iota(jnp.int32, (SIDE, SIDE), 1)
    block_rows = lax.broadcasted_iota(jnp.int32, (block, SIDE), 0)
    block_cols = lax.broadcasted_iota(jnp.int32, (block, SIDE), 1)

    def near_spot(place):
        return pl.ds(pl.multiple_of(place * block, block), block)

    def give(turn, source, target):
        return pltpu.make_async_remote_copy(
            src_ref=sums.at[turn, :, near_spot(target)],
            dst_ref=near_in.at[turn, source],
            send_sem=near_send.at[turn, target],
            recv_sem=near_recv.at[turn, source],
            device_id=at_device(near_device(target)),
            device_id_type=MESH,
        )

    def spread(turn, source, target):
        return pltpu.make_async_remote_copy(
            src_ref=far_in.at[turn, source],
            dst_ref=far_in.at[turn, source],
            send_sem=far_send.at[turn, target],
            recv_sem=far_recv.at[turn, source],
            device_id=at_device(far_device(target)),
            device_id_type=MESH,
        )

    def share(turn, source, target):
        return pltpu.make_async_remote_copy(
            src_ref=grads.at[turn, near_spot(source)],
            dst_ref=grads.at[turn, near_spot(source)],
            send_sem=grad_send.at[turn, target],
            recv_sem=grad_recv.at[turn, source],
            device_id=at_device(near_device(target)),
            device_id_type=MESH,
        )

    def others(own, count, act):
        if count <= 8:
            for step in range(1, count):
                act((own + step) % count)
        else:

            @pl.loop(1, count)
            def _(step):
                act((own + step) % count)

    def reduce_sums(turn, first_task, second_task):
        others(place_near, near, lambda place: give(turn, place_near, place).start())
        first_task()
        total = sums[turn, :, near_spot(place_near), :]
        for step in range(1, near):
            place = (place_near + step) % near
            give(turn, place, place).wait_recv()
            total = total + near_in[turn, place]
        far_in[turn, group_near] = total
        others(group_near, far, lambda group: spread(turn, group_near, group).start())
        second_task()
        others(group_near, far, lambda group: spread(turn, group, group).wait_recv())
        total = far_in[turn, 0]
        if far <= 8:
            for group in range(1, far):
                total = total + far_in[turn, group]
        else:
            total = lax.fori_loop(1, far, lambda group, value: value + far_in[turn, group], total)
        no_first = (block_rows == 0) & (block_cols == 0) & (place_near == 0)
        grads[turn, near_spot(place_near), :] = jnp.where(
            no_first, 0.0, total[0] / (total[1] + epsilon)
        )
        others(place_near, near, lambda place: share(turn, place_near, place).start())
        others(place_near, near, lambda place: share(turn, place, place).wait_recv())
        gradient = grads[turn]
        lower = (row_ids >= col_ids).astype(jnp.float32)
        upper = (row_ids < col_ids).astype(jnp.float32)
        inside = jnp.dot(
            lower, gradient, precision=lax.Precision.HIGHEST, preferred_element_type=jnp.float32
        )
        columns = jnp.broadcast_to(inside[SIDE - 1 :], (8, SIDE))
        before = jnp.dot(
            columns, upper, precision=lax.Precision.HIGHEST, preferred_element_type=jnp.float32
        )
        running = inside + before[:1]
        phase[...] = running if turn == 0 else phase[...] + running

    def drain(turn):
        others(place_near, near, lambda place: give(turn, place_near, place).wait_send())
        others(group_near, far, lambda group: spread(turn, group_near, group).wait_send())
        others(place_near, near, lambda place: share(turn, place_near, place).wait_send())

    def nothing():
        pass

    middle = strong_units // 2
    quarter = strong_units + (units - strong_units) // 4
    halfway = strong_units + (units - strong_units) // 2
    for turn in range(ITERS):
        if turn > 0:
            cosine, sine = jnp.cos(phase[...]), jnp.sin(phase[...])

            @pl.loop(0, strong_units)
            def _(pair):
                value = inverse(correct(hist[pair], cosine, sine), ahead_right, back_left, twist)
                add_terms(turn, pair, value)

        first_task, second_task = nothing, nothing
        if turn == 0:
            first_task = lambda: add_history(0, middle)
            second_task = lambda: add_history(middle, strong_units)
        elif turn == ITERS - 1:
            first_task = lambda: add_history(strong_units, quarter, other_slot)
            second_task = lambda: add_history(quarter, halfway, other_slot)
        reduce_sums(turn, first_task, second_task)

    cosine, sine = jnp.cos(phase[...]), jnp.sin(phase[...])

    def send_out(slot_of, pair, source, target):
        return pltpu.make_async_remote_copy(
            src_ref=ready.at[:, pl.ds(unit * pair, unit), pl.ds(pl.multiple_of(target * depth, depth), depth)],
            dst_ref=landed.at[:, pl.ds(slot_of(pair, source), unit)],
            send_sem=out_send.at[pair, target],
            recv_sem=out_recv.at[pair, source],
            device_id=(rank, target),
            device_id_type=MESH,
        )

    def keep(slot_of, pair):
        return pltpu.make_async_copy(
            ready.at[:, pl.ds(unit * pair, unit), mine],
            landed.at[:, pl.ds(slot_of(pair, part), unit)],
            own_sem.at[pair],
        )

    @pl.loop(0, strong_units)
    def _(pair):
        value = inverse(correct(hist[pair], cosine, sine), ahead_right, back_left, twist)
        for half in range(2):
            for line in range(unit):
                ready[half, unit * pair + line] = value[
                    half * SIDE : (half + 1) * SIDE, line * SIDE : (line + 1) * SIDE
                ]
        for step in order:
            send_out(strong_slot, pair, part, (part + step) % parts).start()
        keep(strong_slot, pair).start()

    def core_rows(which):
        return pl.ds(pl.multiple_of(which * depth, depth), depth)

    def pass_on(pair, source, target):
        return pltpu.make_async_remote_copy(
            src_ref=prepared.at[:, pl.ds(unit * (pair - strong_units), unit), core_rows(target % 2)],
            dst_ref=landed.at[:, pl.ds(other_slot(pair, source), unit)],
            send_sem=pass_send.at[pair - strong_units],
            recv_sem=pass_recv.at[pair - strong_units],
            device_id=(rank, target),
            device_id_type=MESH,
        )

    def keep_other(pair):
        return pltpu.make_async_copy(
            prepared.at[:, pl.ds(unit * (pair - strong_units), unit), core_rows(core)],
            landed.at[:, pl.ds(other_slot(pair, part), unit)],
            own_sem.at[pair],
        )

    def finish_other(pair, spectra):
        value = inverse(correct(spectra, cosine, sine), ahead_right, back_part, twist)
        for half in range(2):
            for line in range(unit):
                prepared[half, unit * (pair - strong_units) + line] = value[
                    half * wide : (half + 1) * wide, line * SIDE : (line + 1) * SIDE
                ]
        pass_on(pair, part, twin).start()
        keep_other(pair).start()

    @pl.loop(strong_units, halfway)
    def _(pair):
        finish_other(pair, hist[pair])

    @pl.loop(halfway, units)
    def _(pair):
        arrived(other_slot, pair)
        finish_other(pair, forward(gathered(pair), ahead_left, back_right, twist))

    for turn in range(ITERS):
        drain(turn)
    turned = phase[...].T
    plain[:SIDE, :] = turned
    phase_out[...] = plain[mine, :]

    @pl.loop(strong_units, units)
    def _(pair):
        for step in order:
            bring(other_slot, pair, part, (part + step) % parts).wait_send()
        pass_on(pair, twin, twin).wait_recv()
        pass_on(pair, part, twin).wait_send()
        keep_other(pair).wait()

    @pl.loop(0, strong_units)
    def _(pair):
        for step in order:
            other = (part + step) % parts
            bring(strong_slot, pair, part, other).wait_send()
            send_out(strong_slot, pair, other, other).wait_recv()
            send_out(strong_slot, pair, part, other).wait_send()
        keep(strong_slot, pair).wait()


def place_rows(
    landed_hbm, places, phase, image_hbm, phase_out, landed, plain, image, load_sem, image_sem
):
    bins = landed.shape[1]
    depth = landed.shape[2]
    groups = bins // 8
    loads = [
        pltpu.make_async_copy(landed_hbm.at[half], landed.at[half], load_sem.at[half])
        for half in range(2)
    ]
    for load in loads:
        load.start()
    phase_out[...] = phase[...]

    def write(half, group):
        spot = pl.ds(pl.multiple_of(group * 8, 8), 8)
        return pltpu.make_async_copy(
            image.at[half, spot], image_hbm.at[half, spot], image_sem.at[half, group]
        )

    for half in range(2):
        loads[half].wait()

        @pl.loop(0, groups)
        def _(group):
            base = (half * bins + group * 8) * depth
            for at in range(8):
                plain[pl.ds(pl.multiple_of(base + at * depth, depth), depth), :] = landed[
                    half, places[group * 8 + at]
                ]
            spot = pl.ds(pl.multiple_of(group * 8, 8), 8)
            for cut in range(depth):
                image[half, spot, cut * SIDE : (cut + 1) * SIDE] = plain[
                    pl.ds(base + cut, 8, stride=depth), :
                ]
            write(half, group).start()

    for half in range(2):

        @pl.loop(0, groups)
        def _(group):
            write(half, group).wait()


def local(ranks, parts, sar_image, strong_index, shifts, widths):
    bins = sar_image.shape[1]
    here = sar_image.shape[2]
    depth = here // SIDE
    strong = strong_index.shape[0]
    devices = ranks * parts
    unit = min(4, strong // parts)
    strong_lines = strong // parts
    other_lines = (bins - strong) // 2
    lines = strong_lines + other_lines
    units = lines // unit
    near = 8
    far = devices // near
    chosen = strong_index % bins
    ids = jnp.arange(bins, dtype=jnp.int32)
    same = chosen[None, :] == ids[:, None]
    ahead = (chosen[None, :] < ids[:, None]).astype(jnp.int32)
    order = jnp.arange(strong, dtype=jnp.int32)[None, :]
    is_strong = jnp.any(same, axis=1)
    slots = jnp.where(
        is_strong,
        jnp.sum(jnp.where(same, order, 0), axis=1),
        strong + ids - jnp.sum(ahead, axis=1),
    )
    located = jnp.sum(jnp.where(slots[None, :] == ids[:, None], ids[None, :], 0), axis=1)
    places = jnp.concatenate([slots, located, shifts, widths])
    tables = make_tables(unit)
    vmem = pl.BlockSpec(memory_space=pltpu.VMEM)
    smem = pl.BlockSpec(memory_space=pltpu.SMEM)
    anywhere = pl.BlockSpec(memory_space=pltpu.HBM)
    dma = pltpu.SemaphoreType.DMA
    landed, phase = pl.pallas_call(
        functools.partial(kernel, ranks, parts, strong),
        out_shape=(
            jax.ShapeDtypeStruct((2, bins, depth, SIDE), jnp.float32),
            jax.ShapeDtypeStruct((depth, SIDE), jnp.float32),
        ),
        in_specs=[anywhere, smem, smem] + [anywhere] * 2,
        out_specs=(anywhere, vmem),
        scratch_shapes=[
            pltpu.VMEM((2, bins, here), jnp.float32),
            pltpu.VMEM(tables[0].shape, jnp.float32),
            pltpu.VMEM((2 * SIDE, 6 * SIDE), jnp.bfloat16),
            pltpu.VMEM((6 * SIDE, 2 * SIDE), jnp.bfloat16),
            pltpu.VMEM((6 * SIDE, 2 * SIDE), jnp.bfloat16),
            pltpu.VMEM((2 * SIDE, 6 * SIDE), jnp.bfloat16),
            pltpu.VMEM((4 * depth, 6 * SIDE), jnp.bfloat16),
            pltpu.VMEM(tables[1].shape, jnp.float32),
            pltpu.VMEM((2 * bins * depth, SIDE), jnp.float32),
            pltpu.VMEM((2, bins, depth, SIDE), jnp.float32),
            pltpu.VMEM((2, bins, depth, SIDE), jnp.float32),
            pltpu.VMEM((2, lines, SIDE, SIDE), jnp.float32),
            pltpu.VMEM((units, unit * SIDE, 2 * SIDE), jnp.float32),
            pltpu.VMEM((ITERS, 2, SIDE, SIDE), jnp.float32),
            pltpu.VMEM((SIDE, SIDE), jnp.float32),
            pltpu.VMEM((ITERS, near, 2, SIDE // near, SIDE), jnp.float32),
            pltpu.VMEM((ITERS, far, 2, SIDE // near, SIDE), jnp.float32),
            pltpu.VMEM((ITERS, SIDE, SIDE), jnp.float32),
            pltpu.VMEM((2, strong_lines, SIDE, SIDE), jnp.float32),
            pltpu.VMEM((2, other_lines, 2 * depth, SIDE), jnp.float32),
            dma((3,)),
            dma((units,)),
            dma((units, parts)),
            dma((units, parts)),
            dma((ITERS, near)),
            dma((ITERS, near)),
            dma((ITERS, far)),
            dma((ITERS, far)),
            dma((ITERS, near)),
            dma((ITERS, near)),
            dma((units, parts)),
            dma((units, parts)),
            dma((other_lines // unit,)),
            dma((other_lines // unit,)),
        ],
        compiler_params=pltpu.CompilerParams(
            collective_id=0, has_side_effects=True, vmem_limit_bytes=56 * 2**20
        ),
        name="autofocus",
    )(sar_image, places, jnp.asarray(make_turns()), *[jnp.asarray(t) for t in tables])
    image, phase = pl.pallas_call(
        place_rows,
        out_shape=(
            jax.ShapeDtypeStruct((2, bins, here), jnp.float32),
            jax.ShapeDtypeStruct((depth, SIDE), jnp.float32),
        ),
        in_specs=[anywhere, smem, vmem],
        out_specs=(anywhere, vmem),
        scratch_shapes=[
            pltpu.VMEM((2, bins, depth, SIDE), jnp.float32),
            pltpu.VMEM((2 * bins * depth, SIDE), jnp.float32),
            pltpu.VMEM((2, bins, here), jnp.float32),
            dma((2,)),
            dma((2, bins // 8)),
        ],
        compiler_params=pltpu.CompilerParams(vmem_limit_bytes=56 * 2**20),
        name="place_rows",
    )(landed, places, phase)
    return image, phase.reshape(here)


def solution(mesh):
    placed = (P(None, "rng", "az"), P("rng"), P("rng"), P("rng"))
    return jax.shard_map(
        functools.partial(local, mesh.shape["rng"], mesh.shape["az"]),
        mesh=mesh,
        in_specs=placed,
        out_specs=(P(None, "rng", "az"), P("az")),
        check_vma=False,
    )
```

```python
import functools
import math

import jax
import jax.numpy as jnp
import numpy as np
from jax import lax
from jax.experimental import pallas as pl
from jax.experimental.pallas import tpu as pltpu
from jax.sharding import PartitionSpec as P

ITERS = 2
SIDE = 128
MESH = pl.DeviceIdType.MESH

epsilon = 1e-06


def make_tables(unit):
    pulses = SIDE * SIDE
    grid = np.arange(SIDE)[:, None] * np.arange(SIDE)[None, :]
    angle = 2.0 * math.pi / SIDE * (grid % SIDE)
    cosine, sine = np.cos(angle), np.sin(angle)
    ahead = np.block([[cosine, sine], [-sine, cosine]])
    back = np.block([[cosine, -sine], [sine, cosine]])
    turn = 2.0 * math.pi / pulses * grid
    twist = np.stack([np.tile(np.cos(turn), (1, unit)), np.tile(np.sin(turn), (1, unit))]) / SIDE
    return np.stack([ahead, back]).astype(np.float32), twist.astype(np.float32)


def make_turns():
    units = np.arange(SIDE)
    coarse = 2.0 * math.pi / SIDE * units
    fine = 2.0 * math.pi / (SIDE * SIDE) * units
    columns = []
    for exact in (-np.cos(coarse), -np.sin(coarse), np.cos(fine), np.sin(fine)):
        high = np.round(exact * 2048.0) / 2048.0
        columns += [high, exact - high]
    return np.concatenate(columns).astype(np.float32)


def line_turn(turns, shift):
    coarse, fine = shift // SIDE, shift % SIDE
    cc_h, cc_l, cs_h, cs_l = [turns[coarse + SIDE * at] for at in range(4)]
    fc_h, fc_l, fs_h, fs_l = [turns[fine + SIDE * at] for at in range(4, 8)]
    cos_h = cc_h * fc_h - cs_h * fs_h
    cos_l = (cc_h * fc_l + cc_l * (fc_h + fc_l)) - (cs_h * fs_l + cs_l * (fs_h + fs_l))
    sin_h = cs_h * fc_h + cc_h * fs_h
    sin_l = (cs_h * fc_l + cs_l * (fc_h + fc_l)) + (cc_h * fs_l + cc_l * (fs_h + fs_l))
    return cos_h, cos_l, sin_h, sin_l


def halves(value):
    high = value.astype(jnp.bfloat16)
    low = (value - high.astype(jnp.float32)).astype(jnp.bfloat16)
    return high, low


def left(matrix_ref, value):
    high, low = halves(value)
    stacked = jnp.concatenate([high, high, low], axis=0)
    return jnp.dot(matrix_ref[...], stacked, preferred_element_type=jnp.float32)


def right(value, matrix_ref):
    high, low = halves(value)
    stacked = jnp.concatenate([high, low, high], axis=1)
    return jnp.dot(stacked, matrix_ref[...], preferred_element_type=jnp.float32)


def lanes_to_rows(real_part, imag_part):
    lines = real_part.shape[1] // SIDE
    spots = [slice(line * SIDE, (line + 1) * SIDE) for line in range(lines)]
    return jnp.concatenate(
        [jnp.concatenate([real_part[:, at], imag_part[:, at]], axis=1) for at in spots], axis=0
    )


def rows_to_lanes(value):
    lines = value.shape[0] // SIDE
    spots = [slice(line * SIDE, (line + 1) * SIDE) for line in range(lines)]
    real_part = jnp.concatenate([value[at, :SIDE] for at in spots], axis=1)
    imag_part = jnp.concatenate([value[at, SIDE:] for at in spots], axis=1)
    return real_part, imag_part


def forward(pair, ahead_left, back_right, twist):
    section = left(ahead_left, pair)
    sec_r, sec_i = section[:SIDE], section[SIDE:]
    cosine, sine = twist[0], twist[1]
    turned = lanes_to_rows(sec_r * cosine + sec_i * sine, sec_i * cosine - sec_r * sine)
    return right(turned, back_right)


def inverse(spectrum, ahead_right, back_left, twist):
    sec_r, sec_i = rows_to_lanes(right(spectrum, ahead_right))
    cosine, sine = twist[0], twist[1]
    turned = jnp.concatenate(
        [sec_r * cosine - sec_i * sine, sec_i * cosine + sec_r * sine], axis=0
    )
    return left(back_left, turned)


def correct(spectrum, cosine, sine):
    rows = []
    for line in range(spectrum.shape[0] // SIDE):
        part = spectrum[line * SIDE : (line + 1) * SIDE]
        real_part, imag_part = part[:, :SIDE], part[:, SIDE:]
        rows.append(
            jnp.concatenate(
                [real_part * cosine + imag_part * sine, imag_part * cosine - real_part * sine],
                axis=1,
            )
        )
    return jnp.concatenate(rows, axis=0)


def previous(value):
    down = pltpu.roll(value, 1, 0)
    top = down[:8]
    wrapped = pltpu.roll(top, 1, 1)
    first = lax.broadcasted_iota(jnp.int32, (8, SIDE), 0) == 0
    return jnp.concatenate([jnp.where(first, wrapped, top), down[8:]], axis=0)


def kernel(
    ranks,
    parts,
    strong,
    sar_hbm,
    places,
    turns,
    matrices_hbm,
    twist_hbm,
    landed,
    phase_out,
    sar,
    matrices,
    ahead_left,
    back_right,
    ahead_right,
    back_left,
    back_part,
    twist,
    plain,
    natural,
    stage,
    rows,
    hist,
    sums,
    phase,
    near_in,
    far_in,
    grads,
    ready,
    prepared,
    load_sem,
    own_sem,
    in_send,
    in_recv,
    near_send,
    near_recv,
    far_send,
    far_recv,
    grad_send,
    grad_recv,
    out_send,
    out_recv,
    pass_send,
    pass_recv,
):
    devices = ranks * parts
    near = near_in.shape[1]
    far = far_in.shape[1]
    block = SIDE // near
    rank = lax.axis_index("rng")
    part = lax.axis_index("az")
    me = rank * parts + part
    lines = rows.shape[1]
    units = hist.shape[0]
    unit = lines // units
    bins = stage.shape[1]
    depth = stage.shape[2]
    core = part % 2
    twin = part + 1 - 2 * core
    wide = 2 * depth
    mine_strong = strong // parts
    mine_other = lines - mine_strong
    strong_units = mine_strong // unit
    ratio = (units - strong_units) // strong_units
    groups = bins // 8
    slot_at, bin_at, shift_at, width_at = 0, bins, 2 * bins, 2 * bins + strong

    loads = [
        pltpu.make_async_copy(source, target, load_sem.at[at])
        for at, (source, target) in enumerate(
            [
                (sar_hbm, sar),
                (matrices_hbm, matrices),
                (twist_hbm, twist),
            ]
        )
    ]
    loads[0].start()

    barrier = pltpu.get_barrier_semaphore()

    def at_device(other):
        return (other // parts, other % parts)

    group_near, place_near = me // near, me % near

    def near_device(place):
        return group_near * near + place

    def far_device(group):
        return group * near + place_near

    greeted = [near_device((place_near + step) % near) for step in range(1, near)]
    if far <= 8:
        greeted += [far_device((group_near + step) % far) for step in range(1, far)]
    if parts > near or near % parts:
        greeted += [rank * parts + (part + step) % parts for step in range(1, parts)]
    for other in greeted:
        pl.semaphore_signal(barrier, inc=1, device_id=at_device(other), device_id_type=MESH)
    awaited = len(greeted)
    if far > 8:
        awaited += far - 1

        @pl.loop(1, far)
        def _(step):
            other = far_device((group_near + step) % far)
            pl.semaphore_signal(barrier, inc=1, device_id=at_device(other), device_id_type=MESH)

    for load in loads[1:]:
        load.start()
    loads[0].wait()

    for half in range(2):

        @pl.loop(0, groups)
        def _(group):
            spot = pl.ds(pl.multiple_of(group * 8, 8), 8)
            for cut in range(depth):
                plain[pl.ds((half * bins + group * 8) * depth + cut, 8, stride=depth), :] = sar[
                    half, spot, cut * SIDE : (cut + 1) * SIDE
                ]
            for at in range(8):
                start = pl.multiple_of((half * bins + group * 8 + at) * depth, depth)
                natural[half, group * 8 + at] = plain[pl.ds(start, depth), :]

    def arrange(first, last):
        @pl.loop(first, last)
        def _(slot):
            source = places[bin_at + slot]
            for half in range(2):
                stage[half, slot] = natural[half, source]

    arrange(0, strong)
    pl.semaphore_wait(barrier, awaited)

    mine = pl.ds(pl.multiple_of(part * depth, depth), depth)

    def strong_slot(pair, owner):
        return mine_strong * owner + unit * pair

    def other_slot(pair, owner):
        return strong + mine_other * (owner % 2) + unit * (pair - strong_units)

    def bring(slot_of, pair, source, target):
        return pltpu.make_async_remote_copy(
            src_ref=stage.at[:, pl.ds(slot_of(pair, target), unit)],
            dst_ref=rows.at[:, pl.ds(unit * pair, unit), pl.ds(pl.multiple_of(source * depth, depth), depth)],
            send_sem=in_send.at[pair, target],
            recv_sem=in_recv.at[pair, source],
            device_id=(rank, target),
            device_id_type=MESH,
        )

    order = sorted(range(1, parts), key=lambda step: abs(step - parts // 2))

    def begin(slot_of, pair):
        for step in order:
            bring(slot_of, pair, part, (part + step) % parts).start()

    def arrived(slot_of, pair):
        for step in order:
            other = (part + step) % parts
            bring(slot_of, pair, other, other).wait_recv()

    @pl.loop(0, strong_units)
    def _(pair):
        begin(strong_slot, pair)

    arrange(strong, bins)
    for half in range(2):

        @pl.loop(0, mine_strong)
        def _(line):
            rows[half, line, mine, :] = stage[half, mine_strong * part + line]

        @pl.loop(0, mine_other)
        def _(line):
            rows[half, mine_strong + line, mine, :] = stage[half, strong + mine_other * core + line]

    sums[...] = jnp.zeros_like(sums)
    cells = (
        lax.broadcasted_iota(jnp.int32, (SIDE, SIDE), 0) * SIDE
        + lax.broadcasted_iota(jnp.int32, (SIDE, SIDE), 1)
    )
    for load in loads[1:]:
        load.wait()
    ahead_h, ahead_l = halves(matrices[0])
    back_h, back_l = halves(matrices[1])
    ahead_left[...] = jnp.concatenate([ahead_h, ahead_l, ahead_h], axis=1)
    back_right[...] = jnp.concatenate([back_h, back_h, back_l], axis=0)
    ahead_right[...] = jnp.concatenate([ahead_h, ahead_h, ahead_l], axis=0)
    back_left[...] = jnp.concatenate([back_h, back_l, back_h], axis=1)
    half_rows = pl.multiple_of((part // 2) * wide, wide)
    part_h, part_l = halves(
        jnp.concatenate(
            [
                matrices[1, pl.ds(half_rows, wide), :],
                matrices[1, pl.ds(pl.multiple_of(SIDE + half_rows, wide), wide), :],
            ],
            axis=0,
        )
    )
    back_part[...] = jnp.concatenate([part_h, part_l, part_h], axis=1)

    def add_terms(turn, pair, value):
        masks = []
        for line in range(unit):
            at = mine_strong * part + pair * unit + line
            width = places[width_at + at]
            offset = (cells - (places[shift_at + at] - width // 2)) & (SIDE * SIDE - 1)
            masks.append((offset < width).astype(jnp.float32))
        mask = jnp.concatenate(masks, axis=1)
        mask = jnp.concatenate([mask, mask], axis=0)
        spectra = forward(value * mask, ahead_left, back_right, twist)
        num = sums[turn, 0]
        den = sums[turn, 1]
        for line in range(unit):
            at = mine_strong * part + pair * unit + line
            cos_h, cos_l, sin_h, sin_l = line_turn(turns, places[shift_at + at])
            spec_r = spectra[line * SIDE : (line + 1) * SIDE, :SIDE]
            spec_i = spectra[line * SIDE : (line + 1) * SIDE, SIDE:]
            prev_r, prev_i = previous(spec_r), previous(spec_i)
            cross_i = prev_r * spec_i - prev_i * spec_r
            cross_r = prev_r * spec_r + prev_i * spec_i
            rest = cross_i * cos_l + cross_r * sin_l
            num = num + ((cross_i * cos_h + cross_r * sin_h) + rest)
            den = den + (spec_r * spec_r + spec_i * spec_i)
        sums[turn, 0] = num
        sums[turn, 1] = den

    def gathered(pair):
        return jnp.concatenate(
            [
                jnp.concatenate([rows[half, pair * unit + at] for at in range(unit)], axis=1)
                for half in range(2)
            ],
            axis=0,
        )

    @pl.loop(0, strong_units)
    def _(pair):
        arrived(strong_slot, pair)
        for at in range(ratio):
            begin(other_slot, strong_units + pair * ratio + at)
        add_terms(0, pair, gathered(pair))

    def add_history(first, last, slot_of=None):
        @pl.loop(first, last)
        def _(pair):
            if slot_of is not None:
                arrived(slot_of, pair)
            hist[pair] = forward(gathered(pair), ahead_left, back_right, twist)

    row_ids = lax.broadcasted_iota(jnp.int32, (SIDE, SIDE), 0)
    col_ids = lax.broadcasted_iota(jnp.int32, (SIDE, SIDE), 1)
    block_rows = lax.broadcasted_iota(jnp.int32, (block, SIDE), 0)
    block_cols = lax.broadcasted_iota(jnp.int32, (block, SIDE), 1)

    def near_spot(place):
        return pl.ds(pl.multiple_of(place * block, block), block)

    def give(turn, source, target):
        return pltpu.make_async_remote_copy(
            src_ref=sums.at[turn, :, near_spot(target)],
            dst_ref=near_in.at[turn, source],
            send_sem=near_send.at[turn, target],
            recv_sem=near_recv.at[turn, source],
            device_id=at_device(near_device(target)),
            device_id_type=MESH,
        )

    def spread(turn, source, target):
        return pltpu.make_async_remote_copy(
            src_ref=far_in.at[turn, source],
            dst_ref=far_in.at[turn, source],
            send_sem=far_send.at[turn, target],
            recv_sem=far_recv.at[turn, source],
            device_id=at_device(far_device(target)),
            device_id_type=MESH,
        )

    def share(turn, source, target):
        return pltpu.make_async_remote_copy(
            src_ref=grads.at[turn, near_spot(source)],
            dst_ref=grads.at[turn, near_spot(source)],
            send_sem=grad_send.at[turn, target],
            recv_sem=grad_recv.at[turn, source],
            device_id=at_device(near_device(target)),
            device_id_type=MESH,
        )

    def others(own, count, act):
        if count <= 8:
            for step in range(1, count):
                act((own + step) % count)
        else:

            @pl.loop(1, count)
            def _(step):
                act((own + step) % count)

    def reduce_sums(turn, first_task, second_task):
        others(place_near, near, lambda place: give(turn, place_near, place).start())
        first_task()
        total = sums[turn, :, near_spot(place_near), :]
        for step in range(1, near):
            place = (place_near + step) % near
            give(turn, place, place).wait_recv()
            total = total + near_in[turn, place]
        far_in[turn, group_near] = total
        others(group_near, far, lambda group: spread(turn, group_near, group).start())
        second_task()
        others(group_near, far, lambda group: spread(turn, group, group).wait_recv())
        total = far_in[turn, 0]
        if far <= 8:
            for group in range(1, far):
                total = total + far_in[turn, group]
        else:
            total = lax.fori_loop(1, far, lambda group, value: value + far_in[turn, group], total)
        no_first = (block_rows == 0) & (block_cols == 0) & (place_near == 0)
        grads[turn, near_spot(place_near), :] = jnp.where(
            no_first, 0.0, total[0] / (total[1] + epsilon)
        )
        others(place_near, near, lambda place: share(turn, place_near, place).start())
        others(place_near, near, lambda place: share(turn, place, place).wait_recv())
        gradient = grads[turn]
        lower = (row_ids >= col_ids).astype(jnp.float32)
        upper = (row_ids < col_ids).astype(jnp.float32)
        inside = jnp.dot(
            lower, gradient, precision=lax.Precision.HIGHEST, preferred_element_type=jnp.float32
        )
        columns = jnp.broadcast_to(inside[SIDE - 1 :], (8, SIDE))
        before = jnp.dot(
            columns, upper, precision=lax.Precision.HIGHEST, preferred_element_type=jnp.float32
        )
        running = inside + before[:1]
        phase[...] = running if turn == 0 else phase[...] + running

    def drain(turn):
        others(place_near, near, lambda place: give(turn, place_near, place).wait_send())
        others(group_near, far, lambda group: spread(turn, group_near, group).wait_send())
        others(place_near, near, lambda place: share(turn, place_near, place).wait_send())

    def nothing():
        pass

    middle = strong_units // 2
    quarter = strong_units + (units - strong_units) // 4
    halfway = strong_units + (units - strong_units) // 2
    for turn in range(ITERS):
        if turn > 0:
            cosine, sine = jnp.cos(phase[...]), jnp.sin(phase[...])

            @pl.loop(0, strong_units, unroll=True)
            def _(pair):
                value = inverse(correct(hist[pair], cosine, sine), ahead_right, back_left, twist)
                add_terms(turn, pair, value)

        first_task, second_task = nothing, nothing
        if turn == 0:
            first_task = lambda: add_history(0, middle)
            second_task = lambda: add_history(middle, strong_units)
        elif turn == ITERS - 1:
            first_task = lambda: add_history(strong_units, quarter, other_slot)
            second_task = lambda: add_history(quarter, halfway, other_slot)
        reduce_sums(turn, first_task, second_task)

    cosine, sine = jnp.cos(phase[...]), jnp.sin(phase[...])

    def send_out(slot_of, pair, source, target):
        return pltpu.make_async_remote_copy(
            src_ref=ready.at[:, pl.ds(unit * pair, unit), pl.ds(pl.multiple_of(target * depth, depth), depth)],
            dst_ref=landed.at[:, pl.ds(slot_of(pair, source), unit)],
            send_sem=out_send.at[pair, target],
            recv_sem=out_recv.at[pair, source],
            device_id=(rank, target),
            device_id_type=MESH,
        )

    def keep(slot_of, pair):
        return pltpu.make_async_copy(
            ready.at[:, pl.ds(unit * pair, unit), mine],
            landed.at[:, pl.ds(slot_of(pair, part), unit)],
            own_sem.at[pair],
        )

    @pl.loop(0, strong_units, unroll=True)
    def _(pair):
        value = inverse(correct(hist[pair], cosine, sine), ahead_right, back_left, twist)
        for half in range(2):
            for line in range(unit):
                ready[half, unit * pair + line] = value[
                    half * SIDE : (half + 1) * SIDE, line * SIDE : (line + 1) * SIDE
                ]

    @pl.loop(0, strong_units)
    def _(pair):
        for step in order:
            send_out(strong_slot, pair, part, (part + step) % parts).start()
        keep(strong_slot, pair).start()

    def core_rows(which):
        return pl.ds(pl.multiple_of(which * depth, depth), depth)

    def pass_on(pair, source, target):
        return pltpu.make_async_remote_copy(
            src_ref=prepared.at[:, pl.ds(unit * (pair - strong_units), unit), core_rows(target % 2)],
            dst_ref=landed.at[:, pl.ds(other_slot(pair, source), unit)],
            send_sem=pass_send.at[pair - strong_units],
            recv_sem=pass_recv.at[pair - strong_units],
            device_id=(rank, target),
            device_id_type=MESH,
        )

    def keep_other(pair):
        return pltpu.make_async_copy(
            prepared.at[:, pl.ds(unit * (pair - strong_units), unit), core_rows(core)],
            landed.at[:, pl.ds(other_slot(pair, part), unit)],
            own_sem.at[pair],
        )

    def finish_other(pair, spectra):
        value = inverse(correct(spectra, cosine, sine), ahead_right, back_part, twist)
        for half in range(2):
            for line in range(unit):
                prepared[half, unit * (pair - strong_units) + line] = value[
                    half * wide : (half + 1) * wide, line * SIDE : (line + 1) * SIDE
                ]

    def deliver_others(first, last):
        @pl.loop(first, last)
        def _(pair):
            pass_on(pair, part, twin).start()
            keep_other(pair).start()

    @pl.loop(strong_units, halfway, unroll=True)
    def _(pair):
        finish_other(pair, hist[pair])

    deliver_others(strong_units, halfway)

    @pl.loop(halfway, units)
    def _(pair):
        arrived(other_slot, pair)

    @pl.loop(halfway, units, unroll=True)
    def _(pair):
        finish_other(pair, forward(gathered(pair), ahead_left, back_right, twist))

    deliver_others(halfway, units)
    for turn in range(ITERS):
        drain(turn)
    turned = phase[...].T
    plain[:SIDE, :] = turned
    phase_out[...] = plain[mine, :]

    @pl.loop(strong_units, units)
    def _(pair):
        for step in order:
            bring(other_slot, pair, part, (part + step) % parts).wait_send()
        pass_on(pair, twin, twin).wait_recv()
        pass_on(pair, part, twin).wait_send()
        keep_other(pair).wait()

    @pl.loop(0, strong_units)
    def _(pair):
        for step in order:
            other = (part + step) % parts
            bring(strong_slot, pair, part, other).wait_send()
            send_out(strong_slot, pair, other, other).wait_recv()
            send_out(strong_slot, pair, part, other).wait_send()
        keep(strong_slot, pair).wait()


def place_rows(
    landed_hbm, places, phase, image_hbm, phase_out, landed, plain, image, load_sem, image_sem
):
    bins = landed.shape[1]
    depth = landed.shape[2]
    groups = bins // 8
    loads = [
        pltpu.make_async_copy(landed_hbm.at[half], landed.at[half], load_sem.at[half])
        for half in range(2)
    ]
    for load in loads:
        load.start()
    phase_out[...] = phase[...]

    def write(half, group):
        spot = pl.ds(pl.multiple_of(group * 8, 8), 8)
        return pltpu.make_async_copy(
            image.at[half, spot], image_hbm.at[half, spot], image_sem.at[half, group]
        )

    for half in range(2):
        loads[half].wait()

        @pl.loop(0, groups)
        def _(group):
            base = (half * bins + group * 8) * depth
            for at in range(8):
                plain[pl.ds(pl.multiple_of(base + at * depth, depth), depth), :] = landed[
                    half, places[group * 8 + at]
                ]
            spot = pl.ds(pl.multiple_of(group * 8, 8), 8)
            for cut in range(depth):
                image[half, spot, cut * SIDE : (cut + 1) * SIDE] = plain[
                    pl.ds(base + cut, 8, stride=depth), :
                ]
            write(half, group).start()

    for half in range(2):

        @pl.loop(0, groups)
        def _(group):
            write(half, group).wait()


def local(ranks, parts, sar_image, strong_index, shifts, widths):
    bins = sar_image.shape[1]
    here = sar_image.shape[2]
    depth = here // SIDE
    strong = strong_index.shape[0]
    devices = ranks * parts
    unit = min(4, strong // parts)
    strong_lines = strong // parts
    other_lines = (bins - strong) // 2
    lines = strong_lines + other_lines
    units = lines // unit
    near = 8
    far = devices // near
    chosen = strong_index % bins
    ids = jnp.arange(bins, dtype=jnp.int32)
    same = chosen[None, :] == ids[:, None]
    ahead = (chosen[None, :] < ids[:, None]).astype(jnp.int32)
    order = jnp.arange(strong, dtype=jnp.int32)[None, :]
    is_strong = jnp.any(same, axis=1)
    slots = jnp.where(
        is_strong,
        jnp.sum(jnp.where(same, order, 0), axis=1),
        strong + ids - jnp.sum(ahead, axis=1),
    )
    located = jnp.sum(jnp.where(slots[None, :] == ids[:, None], ids[None, :], 0), axis=1)
    places = jnp.concatenate([slots, located, shifts, widths])
    tables = make_tables(unit)
    vmem = pl.BlockSpec(memory_space=pltpu.VMEM)
    smem = pl.BlockSpec(memory_space=pltpu.SMEM)
    anywhere = pl.BlockSpec(memory_space=pltpu.HBM)
    dma = pltpu.SemaphoreType.DMA
    landed, phase = pl.pallas_call(
        functools.partial(kernel, ranks, parts, strong),
        out_shape=(
            jax.ShapeDtypeStruct((2, bins, depth, SIDE), jnp.float32),
            jax.ShapeDtypeStruct((depth, SIDE), jnp.float32),
        ),
        in_specs=[anywhere, smem, smem] + [anywhere] * 2,
        out_specs=(anywhere, vmem),
        scratch_shapes=[
            pltpu.VMEM((2, bins, here), jnp.float32),
            pltpu.VMEM(tables[0].shape, jnp.float32),
            pltpu.VMEM((2 * SIDE, 6 * SIDE), jnp.bfloat16),
            pltpu.VMEM((6 * SIDE, 2 * SIDE), jnp.bfloat16),
            pltpu.VMEM((6 * SIDE, 2 * SIDE), jnp.bfloat16),
            pltpu.VMEM((2 * SIDE, 6 * SIDE), jnp.bfloat16),
            pltpu.VMEM((4 * depth, 6 * SIDE), jnp.bfloat16),
            pltpu.VMEM(tables[1].shape, jnp.float32),
            pltpu.VMEM((2 * bins * depth, SIDE), jnp.float32),
            pltpu.VMEM((2, bins, depth, SIDE), jnp.float32),
            pltpu.VMEM((2, bins, depth, SIDE), jnp.float32),
            pltpu.VMEM((2, lines, SIDE, SIDE), jnp.float32),
            pltpu.VMEM((units, unit * SIDE, 2 * SIDE), jnp.float32),
            pltpu.VMEM((ITERS, 2, SIDE, SIDE), jnp.float32),
            pltpu.VMEM((SIDE, SIDE), jnp.float32),
            pltpu.VMEM((ITERS, near, 2, SIDE // near, SIDE), jnp.float32),
            pltpu.VMEM((ITERS, far, 2, SIDE // near, SIDE), jnp.float32),
            pltpu.VMEM((ITERS, SIDE, SIDE), jnp.float32),
            pltpu.VMEM((2, strong_lines, SIDE, SIDE), jnp.float32),
            pltpu.VMEM((2, other_lines, 2 * depth, SIDE), jnp.float32),
            dma((3,)),
            dma((units,)),
            dma((units, parts)),
            dma((units, parts)),
            dma((ITERS, near)),
            dma((ITERS, near)),
            dma((ITERS, far)),
            dma((ITERS, far)),
            dma((ITERS, near)),
            dma((ITERS, near)),
            dma((units, parts)),
            dma((units, parts)),
            dma((other_lines // unit,)),
            dma((other_lines // unit,)),
        ],
        compiler_params=pltpu.CompilerParams(
            collective_id=0, has_side_effects=True, vmem_limit_bytes=56 * 2**20
        ),
        name="autofocus",
    )(sar_image, places, jnp.asarray(make_turns()), *[jnp.asarray(t) for t in tables])
    image, phase = pl.pallas_call(
        place_rows,
        out_shape=(
            jax.ShapeDtypeStruct((2, bins, here), jnp.float32),
            jax.ShapeDtypeStruct((depth, SIDE), jnp.float32),
        ),
        in_specs=[anywhere, smem, vmem],
        out_specs=(anywhere, vmem),
        scratch_shapes=[
            pltpu.VMEM((2, bins, depth, SIDE), jnp.float32),
            pltpu.VMEM((2 * bins * depth, SIDE), jnp.float32),
            pltpu.VMEM((2, bins, here), jnp.float32),
            dma((2,)),
            dma((2, bins // 8)),
        ],
        compiler_params=pltpu.CompilerParams(vmem_limit_bytes=56 * 2**20),
        name="place_rows",
    )(landed, places, phase)
    return image, phase.reshape(here)


def solution(mesh):
    placed = (P(None, "rng", "az"), P("rng"), P("rng"), P("rng"))
    return jax.shard_map(
        functools.partial(local, mesh.shape["rng"], mesh.shape["az"]),
        mesh=mesh,
        in_specs=placed,
        out_specs=(P(None, "rng", "az"), P("az")),
        check_vma=False,
    )
```

```python
import functools
import math

import jax
import jax.numpy as jnp
import numpy as np
from jax import lax
from jax.experimental import pallas as pl
from jax.experimental.pallas import tpu as pltpu
from jax.sharding import PartitionSpec as P

ITERS = 2
SIDE = 128
MESH = pl.DeviceIdType.MESH

epsilon = 1e-06


def make_tables(unit):
    pulses = SIDE * SIDE
    grid = np.arange(SIDE)[:, None] * np.arange(SIDE)[None, :]
    angle = 2.0 * math.pi / SIDE * (grid % SIDE)
    cosine, sine = np.cos(angle), np.sin(angle)
    ahead = np.block([[cosine, sine], [-sine, cosine]])
    back = np.block([[cosine, -sine], [sine, cosine]])
    turn = 2.0 * math.pi / pulses * grid
    twist = np.stack([np.tile(np.cos(turn), (1, unit)), np.tile(np.sin(turn), (1, unit))]) / SIDE
    return np.stack([ahead, back]).astype(np.float32), twist.astype(np.float32)


def make_turns():
    units = np.arange(SIDE)
    coarse = 2.0 * math.pi / SIDE * units
    fine = 2.0 * math.pi / (SIDE * SIDE) * units
    columns = []
    for exact in (-np.cos(coarse), -np.sin(coarse), np.cos(fine), np.sin(fine)):
        high = np.round(exact * 2048.0) / 2048.0
        columns += [high, exact - high]
    return np.concatenate(columns).astype(np.float32)


def line_turn(turns, shift):
    coarse, fine = shift // SIDE, shift % SIDE
    cc_h, cc_l, cs_h, cs_l = [turns[coarse + SIDE * at] for at in range(4)]
    fc_h, fc_l, fs_h, fs_l = [turns[fine + SIDE * at] for at in range(4, 8)]
    cos_h = cc_h * fc_h - cs_h * fs_h
    cos_l = (cc_h * fc_l + cc_l * (fc_h + fc_l)) - (cs_h * fs_l + cs_l * (fs_h + fs_l))
    sin_h = cs_h * fc_h + cc_h * fs_h
    sin_l = (cs_h * fc_l + cs_l * (fc_h + fc_l)) + (cc_h * fs_l + cc_l * (fs_h + fs_l))
    return cos_h, cos_l, sin_h, sin_l


def halves(value):
    high = value.astype(jnp.bfloat16)
    low = (value - high.astype(jnp.float32)).astype(jnp.bfloat16)
    return high, low


def left(matrix_ref, value):
    high, low = halves(value)
    stacked = jnp.concatenate([high, high, low], axis=0)
    return jnp.dot(matrix_ref[...], stacked, preferred_element_type=jnp.float32)


def right(value, matrix_ref):
    high, low = halves(value)
    stacked = jnp.concatenate([high, low, high], axis=1)
    return jnp.dot(stacked, matrix_ref[...], preferred_element_type=jnp.float32)


def lanes_to_rows(real_part, imag_part):
    lines = real_part.shape[1] // SIDE
    spots = [slice(line * SIDE, (line + 1) * SIDE) for line in range(lines)]
    return jnp.concatenate(
        [jnp.concatenate([real_part[:, at], imag_part[:, at]], axis=1) for at in spots], axis=0
    )


def rows_to_lanes(value):
    lines = value.shape[0] // SIDE
    spots = [slice(line * SIDE, (line + 1) * SIDE) for line in range(lines)]
    real_part = jnp.concatenate([value[at, :SIDE] for at in spots], axis=1)
    imag_part = jnp.concatenate([value[at, SIDE:] for at in spots], axis=1)
    return real_part, imag_part


def forward(pair, ahead_left, back_right, twist):
    section = left(ahead_left, pair)
    sec_r, sec_i = section[:SIDE], section[SIDE:]
    cosine, sine = twist[0], twist[1]
    turned = lanes_to_rows(sec_r * cosine + sec_i * sine, sec_i * cosine - sec_r * sine)
    return right(turned, back_right)


def inverse(spectrum, ahead_right, back_left, twist):
    sec_r, sec_i = rows_to_lanes(right(spectrum, ahead_right))
    cosine, sine = twist[0], twist[1]
    turned = jnp.concatenate(
        [sec_r * cosine - sec_i * sine, sec_i * cosine + sec_r * sine], axis=0
    )
    return left(back_left, turned)


def correct(spectrum, cosine, sine):
    rows = []
    for line in range(spectrum.shape[0] // SIDE):
        part = spectrum[line * SIDE : (line + 1) * SIDE]
        real_part, imag_part = part[:, :SIDE], part[:, SIDE:]
        rows.append(
            jnp.concatenate(
                [real_part * cosine + imag_part * sine, imag_part * cosine - real_part * sine],
                axis=1,
            )
        )
    return jnp.concatenate(rows, axis=0)


def previous(value):
    down = pltpu.roll(value, 1, 0)
    top = down[:8]
    wrapped = pltpu.roll(top, 1, 1)
    first = lax.broadcasted_iota(jnp.int32, (8, SIDE), 0) == 0
    return jnp.concatenate([jnp.where(first, wrapped, top), down[8:]], axis=0)


def kernel(
    ranks,
    parts,
    strong,
    sar_hbm,
    places,
    turns,
    matrices_hbm,
    twist_hbm,
    image_hbm,
    phase_out,
    sar,
    matrices,
    ahead_left,
    back_right,
    ahead_right,
    back_left,
    twist,
    plain,
    stage,
    rows,
    hist,
    sums,
    phase,
    near_in,
    far_in,
    grads,
    ready,
    landed,
    image,
    load_sem,
    image_sem,
    in_send,
    in_recv,
    near_send,
    near_recv,
    far_send,
    far_recv,
    grad_send,
    grad_recv,
    out_send,
    out_recv,
):
    devices = ranks * parts
    near = near_in.shape[1]
    far = far_in.shape[1]
    block = SIDE // near
    rank = lax.axis_index("rng")
    part = lax.axis_index("az")
    me = rank * parts + part
    lines = rows.shape[1]
    units = hist.shape[0]
    unit = lines // units
    bins = stage.shape[1]
    depth = stage.shape[2]
    mine_strong = strong // parts
    mine_other = lines - mine_strong
    strong_units = mine_strong // unit
    groups = bins // 8
    slot_at, bin_at, shift_at, width_at = 0, bins, 2 * bins, 2 * bins + strong

    loads = [
        pltpu.make_async_copy(source, target, load_sem.at[at])
        for at, (source, target) in enumerate(
            [
                (sar_hbm, sar),
                (matrices_hbm, matrices),
                (twist_hbm, twist),
            ]
        )
    ]
    loads[0].start()

    barrier = pltpu.get_barrier_semaphore()

    def at_device(other):
        return (other // parts, other % parts)

    group_near, place_near = me // near, me % near

    def near_device(place):
        return group_near * near + place

    def far_device(group):
        return group * near + place_near

    greeted = [near_device((place_near + step) % near) for step in range(1, near)]
    if far <= 8:
        greeted += [far_device((group_near + step) % far) for step in range(1, far)]
    if parts > near or near % parts:
        greeted += [rank * parts + (part + step) % parts for step in range(1, parts)]
    for other in greeted:
        pl.semaphore_signal(barrier, inc=1, device_id=at_device(other), device_id_type=MESH)
    awaited = len(greeted)
    if far > 8:
        awaited += far - 1

        @pl.loop(1, far)
        def _(step):
            other = far_device((group_near + step) % far)
            pl.semaphore_signal(barrier, inc=1, device_id=at_device(other), device_id_type=MESH)

    for load in loads[1:]:
        load.start()
    loads[0].wait()

    for half in range(2):

        @pl.loop(0, groups)
        def _(group):
            spot = pl.ds(pl.multiple_of(group * 8, 8), 8)
            plain[half, spot] = sar[half, spot, :].reshape(8, depth, SIDE)

    def arrange(first, last):
        @pl.loop(first, last)
        def _(slot):
            source = places[bin_at + slot]
            for half in range(2):
                stage[half, slot] = plain[half, source]

    arrange(0, strong)
    pl.semaphore_wait(barrier, awaited)

    mine = pl.ds(pl.multiple_of(part * depth, depth), depth)

    def strong_slot(pair, owner):
        return mine_strong * owner + unit * pair

    def other_slot(pair, owner):
        return strong + mine_other * owner + unit * (pair - strong_units)

    def bring(slot_of, pair, source, target):
        return pltpu.make_async_remote_copy(
            src_ref=stage.at[:, pl.ds(slot_of(pair, target), unit)],
            dst_ref=rows.at[:, pl.ds(unit * pair, unit), pl.ds(pl.multiple_of(source * depth, depth), depth)],
            send_sem=in_send.at[pair, target],
            recv_sem=in_recv.at[pair, source],
            device_id=(rank, target),
            device_id_type=MESH,
        )

    order = sorted(range(1, parts), key=lambda step: abs(step - parts // 2))

    def begin(slot_of, pair):
        for step in order:
            bring(slot_of, pair, part, (part + step) % parts).start()

    def arrived(slot_of, pair):
        for step in order:
            other = (part + step) % parts
            bring(slot_of, pair, other, other).wait_recv()

    @pl.loop(0, strong_units)
    def _(pair):
        begin(strong_slot, pair)

    arrange(strong, bins)
    for half in range(2):

        @pl.loop(0, mine_strong)
        def _(line):
            rows[half, line, mine, :] = stage[half, mine_strong * part + line]

        @pl.loop(0, mine_other)
        def _(line):
            rows[half, mine_strong + line, mine, :] = stage[half, strong + mine_other * part + line]

    sums[...] = jnp.zeros_like(sums)
    cells = (
        lax.broadcasted_iota(jnp.int32, (SIDE, SIDE), 0) * SIDE
        + lax.broadcasted_iota(jnp.int32, (SIDE, SIDE), 1)
    )
    for load in loads[1:]:
        load.wait()
    ahead_h, ahead_l = halves(matrices[0])
    back_h, back_l = halves(matrices[1])
    ahead_left[...] = jnp.concatenate([ahead_h, ahead_l, ahead_h], axis=1)
    back_right[...] = jnp.concatenate([back_h, back_h, back_l], axis=0)
    ahead_right[...] = jnp.concatenate([ahead_h, ahead_h, ahead_l], axis=0)
    back_left[...] = jnp.concatenate([back_h, back_l, back_h], axis=1)

    def add_terms(turn, pair, value):
        masks = []
        for line in range(unit):
            at = mine_strong * part + pair * unit + line
            width = places[width_at + at]
            offset = (cells - (places[shift_at + at] - width // 2)) & (SIDE * SIDE - 1)
            masks.append((offset < width).astype(jnp.float32))
        mask = jnp.concatenate(masks, axis=1)
        mask = jnp.concatenate([mask, mask], axis=0)
        spectra = forward(value * mask, ahead_left, back_right, twist)
        num = sums[turn, 0]
        den = sums[turn, 1]
        for line in range(unit):
            at = mine_strong * part + pair * unit + line
            cos_h, cos_l, sin_h, sin_l = line_turn(turns, places[shift_at + at])
            spec_r = spectra[line * SIDE : (line + 1) * SIDE, :SIDE]
            spec_i = spectra[line * SIDE : (line + 1) * SIDE, SIDE:]
            prev_r, prev_i = previous(spec_r), previous(spec_i)
            cross_i = prev_r * spec_i - prev_i * spec_r
            cross_r = prev_r * spec_r + prev_i * spec_i
            rest = cross_i * cos_l + cross_r * sin_l
            num = num + ((cross_i * cos_h + cross_r * sin_h) + rest)
            den = den + (spec_r * spec_r + spec_i * spec_i)
        sums[turn, 0] = num
        sums[turn, 1] = den

    def gathered(pair):
        return jnp.concatenate(
            [
                jnp.concatenate([rows[half, pair * unit + at] for at in range(unit)], axis=1)
                for half in range(2)
            ],
            axis=0,
        )

    @pl.loop(0, strong_units)
    def _(pair):
        arrived(strong_slot, pair)
        add_terms(0, pair, gathered(pair))

    def add_history(first, last, slot_of=None):
        @pl.loop(first, last)
        def _(pair):
            if slot_of is not None:
                arrived(slot_of, pair)
            hist[pair] = forward(gathered(pair), ahead_left, back_right, twist)

    row_ids = lax.broadcasted_iota(jnp.int32, (SIDE, SIDE), 0)
    col_ids = lax.broadcasted_iota(jnp.int32, (SIDE, SIDE), 1)
    block_rows = lax.broadcasted_iota(jnp.int32, (block, SIDE), 0)
    block_cols = lax.broadcasted_iota(jnp.int32, (block, SIDE), 1)

    def near_spot(place):
        return pl.ds(pl.multiple_of(place * block, block), block)

    def give(turn, source, target):
        return pltpu.make_async_remote_copy(
            src_ref=sums.at[turn, :, near_spot(target)],
            dst_ref=near_in.at[turn, source],
            send_sem=near_send.at[turn, target],
            recv_sem=near_recv.at[turn, source],
            device_id=at_device(near_device(target)),
            device_id_type=MESH,
        )

    def spread(turn, source, target):
        return pltpu.make_async_remote_copy(
            src_ref=far_in.at[turn, source],
            dst_ref=far_in.at[turn, source],
            send_sem=far_send.at[turn, target],
            recv_sem=far_recv.at[turn, source],
            device_id=at_device(far_device(target)),
            device_id_type=MESH,
        )

    def share(turn, source, target):
        return pltpu.make_async_remote_copy(
            src_ref=grads.at[turn, near_spot(source)],
            dst_ref=grads.at[turn, near_spot(source)],
            send_sem=grad_send.at[turn, target],
            recv_sem=grad_recv.at[turn, source],
            device_id=at_device(near_device(target)),
            device_id_type=MESH,
        )

    def others(own, count, act):
        if count <= 8:
            for step in range(1, count):
                act((own + step) % count)
        else:

            @pl.loop(1, count)
            def _(step):
                act((own + step) % count)

    def reduce_sums(turn, first_task, second_task):
        others(place_near, near, lambda place: give(turn, place_near, place).start())
        first_task()
        total = sums[turn, :, near_spot(place_near), :]
        for step in range(1, near):
            place = (place_near + step) % near
            give(turn, place, place).wait_recv()
            total = total + near_in[turn, place]
        far_in[turn, group_near] = total
        others(group_near, far, lambda group: spread(turn, group_near, group).start())
        second_task()
        others(group_near, far, lambda group: spread(turn, group, group).wait_recv())
        total = far_in[turn, 0]
        if far <= 8:
            for group in range(1, far):
                total = total + far_in[turn, group]
        else:
            total = lax.fori_loop(1, far, lambda group, value: value + far_in[turn, group], total)
        no_first = (block_rows == 0) & (block_cols == 0) & (place_near == 0)
        grads[turn, near_spot(place_near), :] = jnp.where(
            no_first, 0.0, total[0] / (total[1] + epsilon)
        )
        others(place_near, near, lambda place: share(turn, place_near, place).start())
        others(place_near, near, lambda place: share(turn, place, place).wait_recv())
        gradient = grads[turn]
        lower = (row_ids >= col_ids).astype(jnp.float32)
        upper = (row_ids < col_ids).astype(jnp.float32)
        inside = jnp.dot(
            lower, gradient, precision=lax.Precision.HIGHEST, preferred_element_type=jnp.float32
        )
        columns = jnp.broadcast_to(inside[SIDE - 1 :], (8, SIDE))
        before = jnp.dot(
            columns, upper, precision=lax.Precision.HIGHEST, preferred_element_type=jnp.float32
        )
        running = inside + before[:1]
        phase[...] = running if turn == 0 else phase[...] + running

    def drain(turn):
        others(place_near, near, lambda place: give(turn, place_near, place).wait_send())
        others(group_near, far, lambda group: spread(turn, group_near, group).wait_send())
        others(place_near, near, lambda place: share(turn, place_near, place).wait_send())

    def nothing():
        pass

    middle = strong_units // 2
    halfway = strong_units + (units - strong_units) // 2
    for turn in range(ITERS):
        if turn == 1:

            @pl.loop(strong_units, units)
            def _(pair):
                begin(other_slot, pair)

        if turn > 0:
            cosine, sine = jnp.cos(phase[...]), jnp.sin(phase[...])

            @pl.loop(0, strong_units)
            def _(pair):
                value = inverse(correct(hist[pair], cosine, sine), ahead_right, back_left, twist)
                add_terms(turn, pair, value)

        first_task, second_task = nothing, nothing
        if turn == 0:
            first_task = lambda: add_history(0, middle)
            second_task = lambda: add_history(middle, strong_units)
        elif turn == ITERS - 1:
            first_task = lambda: add_history(strong_units, halfway, other_slot)
            second_task = lambda: add_history(halfway, units, other_slot)
        reduce_sums(turn, first_task, second_task)

    cosine, sine = jnp.cos(phase[...]), jnp.sin(phase[...])

    def send_out(slot_of, pair, source, target):
        return pltpu.make_async_remote_copy(
            src_ref=ready.at[:, pl.ds(unit * pair, unit), pl.ds(pl.multiple_of(target * depth, depth), depth)],
            dst_ref=landed.at[:, pl.ds(slot_of(pair, source), unit)],
            send_sem=out_send.at[pair, target],
            recv_sem=out_recv.at[pair, source],
            device_id=(rank, target),
            device_id_type=MESH,
        )

    kinds = ((0, strong_units, strong_slot), (strong_units, units, other_slot))
    for first, last, slot_of in kinds:

        @pl.loop(first, last)
        def _(pair):
            value = inverse(correct(hist[pair], cosine, sine), ahead_right, back_left, twist)
            for half in range(2):
                for line in range(unit):
                    ready[half, unit * pair + line] = value[
                        half * SIDE : (half + 1) * SIDE, line * SIDE : (line + 1) * SIDE
                    ]
            for step in order:
                send_out(slot_of, pair, part, (part + step) % parts).start()
            for half in range(2):
                for line in range(unit):
                    landed[half, slot_of(pair, part) + line] = ready[
                        half, unit * pair + line, mine, :
                    ]

    for turn in range(ITERS):
        drain(turn)
    plain[0, : SIDE // depth] = phase[...].T.reshape(SIDE // depth, depth, SIDE)
    phase_out[...] = plain[0, part]

    for first, last, slot_of in kinds:

        @pl.loop(first, last)
        def _(pair):
            for step in order:
                bring(slot_of, pair, part, (part + step) % parts).wait_send()
            for step in order:
                other = (part + step) % parts
                send_out(slot_of, pair, other, other).wait_recv()

    def write(half, group):
        spot = pl.ds(pl.multiple_of(group * 8, 8), 8)
        return pltpu.make_async_copy(
            image.at[half, spot], image_hbm.at[half, spot], image_sem.at[half, group]
        )

    for half in range(2):

        @pl.loop(0, groups)
        def _(group):
            found = [landed[half, places[slot_at + group * 8 + at]] for at in range(8)]
            spot = pl.ds(pl.multiple_of(group * 8, 8), 8)
            image[half, spot, :] = jnp.stack(found).reshape(8, depth * SIDE)
            write(half, group).start()

    for first, last, slot_of in kinds:

        @pl.loop(first, last)
        def _(pair):
            for step in order:
                send_out(slot_of, pair, part, (part + step) % parts).wait_send()

    for half in range(2):

        @pl.loop(0, groups)
        def _(group):
            write(half, group).wait()


def local(ranks, parts, sar_image, strong_index, shifts, widths):
    bins = sar_image.shape[1]
    here = sar_image.shape[2]
    depth = here // SIDE
    lines = bins // parts
    strong = strong_index.shape[0]
    devices = ranks * parts
    unit = min(4, strong // parts)
    units = lines // unit
    near = 8
    far = devices // near
    chosen = strong_index % bins
    ids = jnp.arange(bins, dtype=jnp.int32)
    same = chosen[None, :] == ids[:, None]
    ahead = (chosen[None, :] < ids[:, None]).astype(jnp.int32)
    order = jnp.arange(strong, dtype=jnp.int32)[None, :]
    is_strong = jnp.any(same, axis=1)
    slots = jnp.where(
        is_strong,
        jnp.sum(jnp.where(same, order, 0), axis=1),
        strong + ids - jnp.sum(ahead, axis=1),
    )
    located = jnp.sum(jnp.where(slots[None, :] == ids[:, None], ids[None, :], 0), axis=1)
    places = jnp.concatenate([slots, located, shifts, widths])
    tables = make_tables(unit)
    vmem = pl.BlockSpec(memory_space=pltpu.VMEM)
    smem = pl.BlockSpec(memory_space=pltpu.SMEM)
    anywhere = pl.BlockSpec(memory_space=pltpu.HBM)
    dma = pltpu.SemaphoreType.DMA
    image, phase = pl.pallas_call(
        functools.partial(kernel, ranks, parts, strong),
        out_shape=(
            jax.ShapeDtypeStruct((2, bins, here), jnp.float32),
            jax.ShapeDtypeStruct((depth, SIDE), jnp.float32),
        ),
        in_specs=[anywhere, smem, smem] + [anywhere] * 2,
        out_specs=(anywhere, vmem),
        scratch_shapes=[
            pltpu.VMEM((2, bins, here), jnp.float32),
            pltpu.VMEM(tables[0].shape, jnp.float32),
            pltpu.VMEM((2 * SIDE, 6 * SIDE), jnp.bfloat16),
            pltpu.VMEM((6 * SIDE, 2 * SIDE), jnp.bfloat16),
            pltpu.VMEM((6 * SIDE, 2 * SIDE), jnp.bfloat16),
            pltpu.VMEM((2 * SIDE, 6 * SIDE), jnp.bfloat16),
            pltpu.VMEM(tables[1].shape, jnp.float32),
            pltpu.VMEM((2, bins, depth, SIDE), jnp.float32),
            pltpu.VMEM((2, bins, depth, SIDE), jnp.float32),
            pltpu.VMEM((2, lines, SIDE, SIDE), jnp.float32),
            pltpu.VMEM((units, unit * SIDE, 2 * SIDE), jnp.float32),
            pltpu.VMEM((ITERS, 2, SIDE, SIDE), jnp.float32),
            pltpu.VMEM((SIDE, SIDE), jnp.float32),
            pltpu.VMEM((ITERS, near, 2, SIDE // near, SIDE), jnp.float32),
            pltpu.VMEM((ITERS, far, 2, SIDE // near, SIDE), jnp.float32),
            pltpu.VMEM((ITERS, SIDE, SIDE), jnp.float32),
            pltpu.VMEM((2, lines, SIDE, SIDE), jnp.float32),
            pltpu.VMEM((2, bins, depth, SIDE), jnp.float32),
            pltpu.VMEM((2, bins, here), jnp.float32),
            dma((3,)),
            dma((2, bins // 8)),
            dma((units, parts)),
            dma((units, parts)),
            dma((ITERS, near)),
            dma((ITERS, near)),
            dma((ITERS, far)),
            dma((ITERS, far)),
            dma((ITERS, near)),
            dma((ITERS, near)),
            dma((units, parts)),
            dma((units, parts)),
        ],
        compiler_params=pltpu.CompilerParams(
            collective_id=0, has_side_effects=True, vmem_limit_bytes=56 * 2**20
        ),
        name="autofocus",
    )(sar_image, places, jnp.asarray(make_turns()), *[jnp.asarray(t) for t in tables])
    return image, phase.reshape(here)


def solution(mesh):
    placed = (P(None, "rng", "az"), P("rng"), P("rng"), P("rng"))
    return jax.shard_map(
        functools.partial(local, mesh.shape["rng"], mesh.shape["az"]),
        mesh=mesh,
        in_specs=placed,
        out_specs=(P(None, "rng", "az"), P("az")),
        check_vma=False,
    )
```
